512 devices in a mesh: grp: 16 (over y, core), row: 32 (over x, z).
Axes of the slice: x: 4, y: 8, z: 8, core: 2. Of those that a mesh axis runs over, the one named last changes fastest.
Arguments:
- amplitudes: float32 [8192, 4096], P('grp', 'row'), may hold values from -6 to 6
- dressing: float32 [4096, 4096], P(None, 'row'), may hold values from -0.09375 to 0.09375
- pair_factor: float32 [128, 512, 64], P('grp'), may hold values from -0.25 to 0.25
- blocks: float32 [32, 512, 4096], P('grp', None, 'row'), may hold values from -6 to 6
- pair_block: int32 [128], replicated, may hold values from 0 to 31, as said below
- block_home: int32 [32], replicated, may hold values from 0 to 31, as said below
- tile_mask: int32 [128, 64], P('grp', 'row'), may hold values 0 or 1
- row_energy: float32 [8192], P('grp'), may hold values from 0.5 to 2
- column_energy: float32 [4096], P('row'), may hold values from 0.5 to 2
Outputs:
- residual: float32 [8192, 4096], P('grp', 'row')
- new_amplitudes: float32 [8192, 4096], P('grp', 'row')
The draws below stay inside these ranges and needn't reach their ends.
Inputs may be any that keep to these rules, and one draw needn't show every extreme that they name: Block b is stored at position block_home[b] of blocks; block_home is a permutation, and the owner of block b is block_home[b] // 2. Pair domain p uses block pair_block[p]; the 8 pair domains g * 8 to g * 8 + 7 use blocks of 8 different owners, and pair domains of one group whose blocks have the same owner use the same block.
All inputs are finite; a program needn't handle non-finite values. No bound on the sum of `tile_mask` on one device may be relied on, other than what follows from the above.
Results may differ from the reference program's by a relative error of at most 0.000057.
Values sent between devices are 32-bit elements; how exact they have to be, the bound alone decides.
No kernel may reach another device: no remote copies, remote signals or barrier semaphores. Data moves between devices by JAX's collectives and lax.ppermute only.
A program may use at most 64 MiB of HBM per device.

```python
import math
import jax
import jax.numpy as jnp
from jax import lax

TILE = 64
V = 4096
NAUX = 512
PAIR_DEV = 8
BLK_DEV = 2
NPAIR = 128
NBLK = 32
NCT = 64
M = 8192


def shared_positions(key):
    return jax.random.permutation(key, NBLK).astype(jnp.int32)


def draw_block_home(key, part):
    positions = shared_positions(key)
    return positions


def draw_pair_block(key, part):
    positions = shared_positions(key)
    key = jax.random.fold_in(key, 2)
    groups = NPAIR // PAIR_DEV
    owner_total = NBLK // BLK_DEV
    owner_keys = jax.random.split(key, groups + 1)
    owners = jax.vmap(lambda single: jax.random.permutation(single, owner_total))(owner_keys[:groups])
    local = jax.random.randint(owner_keys[groups], (groups, owner_total), 0, BLK_DEV)
    which = jnp.arange(PAIR_DEV, dtype=jnp.int32) % owner_total
    chosen_owner = jnp.take(owners, which, axis=1)
    chosen_local = jnp.take(local, which, axis=1)
    slots = (chosen_owner * BLK_DEV + chosen_local).reshape(-1).astype(jnp.int32)
    inverse = jnp.argsort(positions).astype(jnp.int32)
    return jnp.take(inverse, slots).astype(jnp.int32)


def plant(result, rng, smallest, largest):
    longest = result.shape.index(max(result.shape))
    spots = []
    for shift in (0, 1):
        where = [jax.random.randint(jax.random.fold_in(rng, axis), (), 0, length) for axis, length in enumerate(result.shape)]
        where[longest] = (where[longest] + shift) % result.shape[longest]
        spots.append(tuple(where))
    return result.at[spots[0]].set(smallest).at[spots[1]].set(largest)


def level_of(stream_key, dims, shards, least, top_value):
    factor_of, own = 1.0, jax.random.fold_in(stream_key, 6)
    for axis_at, blocks in shards:
        heights = jnp.exp(jax.random.uniform(jax.random.fold_in(own, axis_at), (blocks,), jnp.float32, least / len(shards), top_value / len(shards)))
        factor_of = factor_of * jnp.repeat(heights, dims[axis_at] // blocks).reshape([-1 if axis == axis_at else 1 for axis in range(len(dims))])
    return factor_of


def scatter_about(own_key, shape, deviation, most, cuts=(), held_as=jnp.bfloat16):
    result = jax.random.normal(own_key, shape, jnp.float32) * deviation
    if len(cuts) > 0:
        result = level_of(own_key, shape, cuts, -0.22, 0.18) * result
    return jnp.clip(result, min=-most, max=most).astype(held_as)


def setup_inputs(seed: int = 0) -> dict:
    key_list = jax.random.split(jax.random.key(seed), 10)
    return {
        "amplitudes": scatter_about(key_list[0], (M, V), 1.0, 6.0, ((0, 16), (1, 32)), jnp.float32),
        "dressing": scatter_about(key_list[1], (V, V), V ** -0.5, 0.09375, ((1, 32),), jnp.float32),
        "pair_factor": scatter_about(key_list[2], (NPAIR, NAUX, TILE), NAUX ** -0.5, 0.25, ((0, 16),), jnp.float32),
        "blocks": scatter_about(key_list[3], (NBLK, NAUX, V), 1.0, 6.0, ((0, 16), (2, 32)), jnp.float32),
        "pair_block": draw_pair_block(jax.random.fold_in(key_list[9], 71), 0),
        "block_home": draw_block_home(jax.random.fold_in(key_list[9], 71), 0),
        "tile_mask": plant((jax.random.randint(key_list[6], (NPAIR, NCT), 0, 2) < 1).astype(jnp.int32), jax.random.fold_in(key_list[6], 1), 0, 1),
        "row_energy": jnp.clip(jnp.exp(math.log(2.0) - 1.3862944 * jax.random.uniform(key_list[7], (M,), jnp.float32) ** level_of(key_list[7], (M,), ((0, 16),), -0.2, 0.2)), 0.5, 2.0),
        "column_energy": jnp.clip(jnp.exp(math.log(2.0) - 1.3862944 * jax.random.uniform(key_list[8], (V,), jnp.float32) ** level_of(key_list[8], (V,), ((0, 32),), -0.2, 0.2)), 0.5, 2.0),
    }


def reference(amplitudes, dressing, pair_factor, blocks, pair_block, block_home, tile_mask, row_energy, column_energy):
    highest = lax.Precision.HIGHEST
    dressed = jnp.dot(amplitudes, dressing, precision=highest, preferred_element_type=jnp.float32)
    pair_homes = jnp.take(block_home, pair_block).astype(jnp.int32)

    def one_pair(pair_args):
        factor, position = pair_args
        block = lax.dynamic_index_in_dim(blocks, position, 0, keepdims=False)
        return jnp.dot(factor.T, block, precision=highest, preferred_element_type=jnp.float32)

    integral = lax.map(one_pair, (pair_factor, pair_homes))
    column_mask = jnp.repeat(tile_mask.astype(jnp.float32), TILE, axis=1)
    integral = integral * column_mask[:, None, :]
    residual = integral.reshape(NPAIR * TILE, V) + dressed
    denominator = row_energy[:, None] + column_energy[None, :]
    return residual, amplitudes - residual / denominator
```

```python
import jax
import jax.numpy as jnp
from jax import lax
from jax.experimental import pallas as pl
from jax.experimental.pallas import tpu as pltpu
from jax.sharding import Mesh
from jax.sharding import PartitionSpec as P

MIB = 1024 * 1024


def split(value):
    high = value.astype(jnp.bfloat16)
    low = (value - high.astype(jnp.float32)).astype(jnp.bfloat16)
    return high, low


def dot3(left, right):
    one = lambda a, b: jnp.dot(a, b, preferred_element_type=jnp.float32)
    return one(left[0], right[0]) + (one(left[0], right[1]) + one(left[1], right[0]))


def partial_kernel(pieces, z_ref, *refs):
    amps = refs[:pieces]
    panels = refs[pieces : pieces + 4]
    outs = refs[pieces + 4 : pieces + 8]
    high, low = refs[pieces + 8 :]
    z = z_ref[0]
    depth = amps[0].shape[1]
    for k in range(pieces):
        shift = -k if k <= pieces // 2 else k - pieces // 2
        at = lax.rem(z + shift + pieces, pieces) * depth
        at = pl.multiple_of(at, depth)
        h, l = split(amps[k][...])
        high[:, pl.ds(at, depth)] = h
        low[:, pl.ds(at, depth)] = l
    left = (high[...], low[...])
    for k in range(0, 4, 2):
        right = split(jnp.concatenate([panels[k][...], panels[k + 1][...]], axis=1))
        both = dot3(left, right)
        width = both.shape[1] // 2
        outs[k][...] = both[:, :width]
        outs[k + 1][...] = both[:, width:]


def final_kernel(
    home_ref, mask_ref, factor_ref, block_ref, amp_ref, p0, p1, p2, p3, row_ref, col_ref, res_ref, new_ref
):
    k = pl.program_id(0)
    integral = dot3(split(factor_ref[0]), split(block_ref[0]))
    tile = integral.shape[0]
    lane = lax.broadcasted_iota(jnp.int32, integral.shape, 1)
    first = mask_ref[2 * k].astype(jnp.float32)
    second = mask_ref[2 * k + 1].astype(jnp.float32)
    integral = integral * jnp.where(lane < tile, first, second)
    residual = integral + ((p0[...] + p1[...]) + (p2[...] + p3[...]))
    res_ref[...] = residual
    new_ref[...] = amp_ref[...] - residual / (row_ref[...] + col_ref[...])


def shards(
    amplitudes,
    dressing,
    pair_factor,
    blocks,
    pair_block,
    block_home,
    tile_mask,
    row_energy,
    column_energy,
):
    f32 = jnp.float32
    ny, nc = lax.axis_size("y"), lax.axis_size("core")
    nx, nz = lax.axis_size("x"), lax.axis_size("z")
    x, z = lax.axis_index("x"), lax.axis_index("z")
    pair_count, naux, tile = pair_factor.shape
    rows, width = amplitudes.shape

    def shift(value, axis, step):
        n = lax.axis_size(axis)
        return lax.ppermute(value, axis, [(i, (i + step) % n) for i in range(n)])

    portion = lax.all_gather(blocks, ("y", "core"), axis=0, tiled=True)

    depth = nz * width
    panels = []
    for s in range(nx):
        part = lax.dynamic_slice_in_dim(dressing, lax.rem(x + s, nx) * depth, depth)
        panels.append(part if s == 0 else shift(part, "x", s))

    back, ahead = [amplitudes], [amplitudes]
    for s in range(nz // 2):
        back.append(shift(back[-1], "z", 1))
        if s < nz - 1 - nz // 2:
            ahead.append(shift(ahead[-1], "z", -1))
    pieces = back + ahead[1:]

    vmem = pl.BlockSpec(memory_space=pltpu.VMEM)
    smem = pl.BlockSpec(memory_space=pltpu.SMEM)
    partials = pl.pallas_call(
        lambda *refs: partial_kernel(nz, *refs),
        out_shape=[jax.ShapeDtypeStruct((rows, width), f32)] * nx,
        in_specs=[smem] + [vmem] * (nz + nx),
        out_specs=[vmem] * nx,
        scratch_shapes=[pltpu.VMEM((rows, depth), jnp.bfloat16)] * 2,
        compiler_params=pltpu.CompilerParams(vmem_limit_bytes=40 * MIB),
        cost_estimate=pl.CostEstimate(
            flops=6 * rows * depth * width * nx,
            bytes_accessed=4 * (rows * depth + depth * width * nx + rows * width * nx),
            transcendentals=0,
        ),
        name="dressed_partials",
    )(z[None], *pieces, *panels)
    sums = [partials[0]] + [shift(partials[s], "x", -s) for s in range(1, nx)]

    group = lax.axis_index("y") * nc + lax.axis_index("core")
    mine = lax.dynamic_slice_in_dim(pair_block, group * pair_count, pair_count)
    homes = jnp.sum(
        jnp.where(mine[:, None] == jnp.arange(block_home.shape[0])[None, :], block_home[None, :], 0), axis=1
    )
    part = pl.BlockSpec((tile, width), lambda k, home, mask: (k, 0))
    residual, new = pl.pallas_call(
        final_kernel,
        out_shape=[jax.ShapeDtypeStruct((rows, width), f32)] * 2,
        grid_spec=pltpu.PrefetchScalarGridSpec(
            num_scalar_prefetch=2,
            grid=(pair_count,),
            in_specs=[
                pl.BlockSpec((1, tile, naux), lambda k, home, mask: (k, 0, 0)),
                pl.BlockSpec((1, naux, width), lambda k, home, mask: (home[k], 0, 0)),
                part,
                part,
                part,
                part,
                part,
                pl.BlockSpec((tile, 1), lambda k, home, mask: (k, 0)),
                pl.BlockSpec((1, width), lambda k, home, mask: (0, 0)),
            ],
            out_specs=[part, part],
        ),
        compiler_params=pltpu.CompilerParams(vmem_limit_bytes=40 * MIB),
        cost_estimate=pl.CostEstimate(
            flops=6 * rows * naux * width,
            bytes_accessed=4 * (rows * naux + pair_count * naux * width + 7 * rows * width),
            transcendentals=0,
        ),
        name="integral_update",
    )(
        homes,
        tile_mask.reshape(-1),
        jnp.swapaxes(pair_factor, 1, 2),
        portion,
        amplitudes,
        *sums,
        row_energy[:, None],
        column_energy[None, :],
    )
    return residual, new


def solution(mesh):
    sizes = dict(zip(("y", "core", "x", "z"), (8, 2, 4, 8)))
    fine = Mesh(mesh.devices.reshape(tuple(sizes.values())), tuple(sizes))
    grp, row = ("y", "core"), ("x", "z")
    placed = (
        P(grp, row),
        P(None, row),
        P(grp, None, None),
        P(grp, None, row),
        P(),
        P(),
        P(grp, row),
        P(grp),
        P(row),
    )
    return jax.shard_map(
        shards,
        mesh=fine,
        in_specs=placed,
        out_specs=(P(grp, row), P(grp, row)),
        check_vma=False,
    )
```

```python
import jax
import jax.numpy as jnp
from jax import lax
from jax.experimental import pallas as pl
from jax.experimental.pallas import tpu as pltpu
from jax.sharding import Mesh
from jax.sharding import PartitionSpec as P

F32 = jnp.float32
PARAMS = pltpu.CompilerParams(vmem_limit_bytes=48 * 1024 * 1024)
ANY = pl.BlockSpec(memory_space=pl.ANY)
VMEM = pl.BlockSpec(memory_space=pltpu.VMEM)
SMEM = pl.BlockSpec(memory_space=pltpu.SMEM)
FAR = 4


def split(value):
    high = value.astype(jnp.bfloat16)
    low = (value - high.astype(F32)).astype(jnp.bfloat16)
    return high, low


def dot3(left, right):
    one = lambda a, b: jnp.dot(a, b, preferred_element_type=F32)
    return one(left[0], right[0]) + (one(left[0], right[1]) + one(left[1], right[0]))


def start_all(copies, sems):
    made = [pltpu.make_async_copy(src, dst, sems.at[i]) for i, (src, dst) in enumerate(copies)]
    for copy in made:
        copy.start()
    return made


def behind(index, size, core, step):
    return lax.rem(index + jnp.where(core == 0, size - step, step), size)


def cut_kernel(nx, nz, width, dressing, *refs):
    outs, sems = refs[: nx - 1], refs[nx - 1]
    core, x, z = lax.axis_index("core"), lax.axis_index("x"), lax.axis_index("z")
    copies = []
    for s in range(1, nx):
        to = lax.rem(x + s, nx)
        for t in range(FAR + 1):
            row = pl.multiple_of((to * nz + behind(z, nz, core, t)) * width, width)
            copies.append((dressing.at[pl.ds(row, width)], outs[s - 1].at[pl.ds(t * width, width)]))
    for copy in start_all(copies, sems):
        copy.wait()


def partial_kernel(nx, nz, steps, added, *refs):
    count = len(steps)
    pieces, refs = refs[:count], refs[count:]
    dressing, panels, refs = refs[0], refs[1:nx], refs[nx:]
    plus, refs = (refs[0], refs[1:]) if added else (None, refs)
    outs, refs = (refs[:nx], refs[nx:]) if added else (refs[:1], refs[1:])
    amps, dress, sems = refs[:3]
    core, x, z = lax.axis_index("core"), lax.axis_index("x"), lax.axis_index("z")
    width = pieces[0].shape[1]
    first = steps[0] * width
    copies = []
    for s in range(1, nx):
        src = panels[s - 1].at[pl.ds(first, count * width)]
        copies.append((src, dress.at[:, pl.ds(s * width, width)]))
    for k, t in enumerate(steps):
        row = pl.multiple_of((x * nz + behind(z, nz, core, t)) * width, width)
        copies.append((dressing.at[pl.ds(row, width)], dress.at[pl.ds(k * width, width), pl.ds(0, width)]))
    for k in range(count):
        copies.append((pieces[k], amps.at[:, pl.ds(k * width, width)]))
    if added:
        copies.append((plus, refs[3]))
    made = start_all(copies, sems)
    for copy in made[: len(made) - (1 if added else 0)]:
        copy.wait()
    left = split(amps[...])
    for s in range(0, nx, 2):
        both = dot3(left, split(dress[:, s * width : (s + 2) * width]))
        if added and s == 0:
            made[-1].wait()
        for k in range(2):
            value = both[:, k * width : (k + 1) * width]
            if added:
                value = value + refs[3][s + k]
                outs[s + k][...] = value
            else:
                outs[0][s + k] = value


def home_of(pair, pair_block, block_home):
    home = block_home[pair_block[pair]]
    return lax.div(home, 4), lax.rem(lax.div(home, 2), 2), lax.rem(home, 2)


def pick_kernel(ny, pairs, pair_block, block_home, same, cross, out, sems):
    y, core = lax.axis_index("y"), lax.axis_index("core")
    to = behind(y, ny, 1 - core, 1)
    source = behind(to, ny, core, FAR)
    group = to * 2 + core

    def look(i, found):
        at_y, at_core, which = home_of(group * pairs + i, pair_block, block_home)
        hit = at_y == source
        return (
            jnp.where(jnp.logical_and(hit, at_core == core), which, found[0]),
            jnp.where(jnp.logical_and(hit, at_core != core), which, found[1]),
        )

    a, b = lax.fori_loop(0, pairs, look, (jnp.int32(0), jnp.int32(0)))
    for copy in start_all([(same.at[a], out.at[0]), (cross.at[b], out.at[1])], sems):
        copy.wait()


def factor_dot(factor, block):
    high, low = split(factor)
    block_high, block_low = split(block)
    rows = factor.shape[0]
    both = jnp.dot(jnp.concatenate([high, low], axis=0), block_high, preferred_element_type=F32)
    return both[:rows] + (both[rows:] + jnp.dot(high, block_low, preferred_element_type=F32))


def near_kernel(ny, pairs, pair_block, block_home, mine, theirs, *refs):
    sources, refs = refs[: 2 * FAR - 1], refs[2 * FAR - 1 :]
    out_mine, out_theirs, factors, held, factor_sems, sems = refs
    y, core = lax.axis_index("y"), lax.axis_index("core")
    loads = start_all([(mine, factors.at[0]), (theirs, factors.at[1])], factor_sems)

    def source_of(n):
        whose, i = lax.div(n, pairs), lax.rem(n, pairs)
        group = y * 2 + jnp.where(whose == 0, core, 1 - core)
        at_y, at_core, which = home_of(group * pairs + i, pair_block, block_home)
        step = lax.rem(jnp.where(core == 0, y - at_y, at_y - y) + ny, ny)
        same = at_core == core
        far = jnp.where(step < FAR, jnp.where(same, step, step + FAR - 1), -1)
        return jnp.where(step == 0, jnp.where(same, 0, -1), far), which

    def fetch(n, carry):
        source, which = source_of(n)
        for k, ref in enumerate(sources):

            @pl.when(source == k)
            def _():
                pltpu.make_async_copy(ref.at[which], held.at[n], sems.at[n]).start()

        return carry

    lax.fori_loop(0, 2 * pairs, fetch, 0)
    for load in loads:
        load.wait()
    tile = factors.shape[2]
    for whose, out in enumerate((out_mine, out_theirs)):

        def work(i, carry):
            n = whose * pairs + i
            source, which = source_of(n)
            rows = pl.ds(pl.multiple_of(i * tile, tile), tile)

            @pl.when(source >= 0)
            def _():
                pltpu.make_async_copy(sources[0].at[0], held.at[n], sems.at[n]).wait()
                out[rows] = factor_dot(factors[whose, i], held[n])

            @pl.when(source < 0)
            def _():
                out[rows] = jnp.zeros((tile, out.shape[1]), F32)

            return carry

        lax.fori_loop(0, pairs, work, 0)


def last_kernel(
    ny, pairs, pair_block, block_home, mask, factor, far, mine, theirs, s0, s1, s2, s3, amps, row, col, *refs
):
    residual, new, factors, blocks, parts, sems = refs
    y, core = lax.axis_index("y"), lax.axis_index("core")
    copies = [(far, blocks), (factor, factors)]
    copies += [(ref, parts.at[k]) for k, ref in enumerate((mine, theirs, s0, s1, s2, s3, amps))]
    made = start_all(copies, sems)
    for copy in made:
        copy.wait()
    tile = factors.shape[1]
    width = new.shape[1]
    lane = lax.broadcasted_iota(jnp.int32, (tile, width), 1)

    def work(i, carry):
        at_y, at_core, which = home_of((y * 2 + core) * pairs + i, pair_block, block_home)
        rows = pl.ds(pl.multiple_of(i * tile, tile), tile)

        @pl.when(at_y == lax.rem(y + FAR, ny))
        def _():
            entry = jnp.where(at_core == core, 0, 1)
            parts[0, rows] = factor_dot(factors[i], blocks[entry])

        integral = parts[0, rows] + parts[1, rows]
        on = jnp.where(lane < tile, mask[2 * i], mask[2 * i + 1]).astype(F32)
        total = integral * on + ((parts[2, rows] + parts[3, rows]) + (parts[4, rows] + parts[5, rows]))
        residual[rows] = total
        new[rows] = parts[6, rows] - total / (row[rows] + col[...])
        return carry

    lax.fori_loop(0, pairs, work, 0)


def shards(
    amplitudes,
    dressing,
    pair_factor,
    blocks,
    pair_block,
    block_home,
    tile_mask,
    row_energy,
    column_energy,
):
    ny, nx, nz = lax.axis_size("y"), lax.axis_size("x"), lax.axis_size("z")
    pairs, naux, tile = pair_factor.shape
    rows, width = amplitudes.shape
    sem = pltpu.SemaphoreType.DMA

    def ring(value, axis, cross=False):
        n = lax.axis_size(axis)
        names, at = (("y", "core"), lambda c, i: i * 2 + c) if axis == "y" else (("core", axis), lambda c, i: c * n + i)
        pairs_of = []
        for to in range(2):
            for i in range(n):
                pairs_of.append((at(1 - to if cross else to, i), at(to, (i + (1, -1)[to]) % n)))
        return lax.ppermute(value, names, pairs_of)

    def swap(value):
        return lax.ppermute(value, "core", [(0, 1), (1, 0)])

    def shift(value, step):
        return lax.ppermute(value, "x", [(i, (i + step) % nx) for i in range(nx)])

    def chain(value, axis):
        same, cross = [ring(value, axis)], [ring(value, axis, cross=True)]
        for _ in range(FAR - 2):
            same.append(ring(same[-1], axis))
            cross.append(ring(cross[-1], axis))
        return same, cross

    amp_same, amp_cross = chain(amplitudes, "z")
    amp_far = ring(amp_same[-1], "z")
    blk_same, blk_cross = chain(blocks, "y")

    cuts = pl.pallas_call(
        lambda *refs: cut_kernel(nx, nz, width, *refs),
        out_shape=[jax.ShapeDtypeStruct(((FAR + 1) * width, width), F32)] * (nx - 1),
        in_specs=[ANY],
        out_specs=[ANY] * (nx - 1),
        scratch_shapes=[sem(((nx - 1) * (FAR + 1),))],
        compiler_params=PARAMS,
        name="cut",
    )(dressing)
    panels = [shift(cuts[s - 1], s) for s in range(1, nx)]
    factor = jnp.swapaxes(pair_factor, 1, 2)
    factor_other = swap(factor)

    def partial(pieces, steps, plus):
        count = len(steps)
        shape = jax.ShapeDtypeStruct((rows, width), F32)
        scratch = [
            pltpu.VMEM((rows, count * width), F32),
            pltpu.VMEM((count * width, nx * width), F32),
            sem((2 * count + nx,)),
        ]
        if plus is None:
            shape = [jax.ShapeDtypeStruct((nx, rows, width), F32)]
        else:
            shape = [shape] * nx
            scratch.append(pltpu.VMEM((nx, rows, width), F32))
        return pl.pallas_call(
            lambda *refs: partial_kernel(nx, nz, steps, plus is not None, *refs),
            out_shape=shape,
            in_specs=[ANY] * (count + nx + (plus is not None)),
            out_specs=[VMEM] * len(shape),
            scratch_shapes=scratch,
            compiler_params=PARAMS,
            cost_estimate=pl.CostEstimate(
                flops=6 * rows * count * width * nx * width, bytes_accessed=4 * 2 * rows * nx * width, transcendentals=0
            ),
            name="partial_own" if plus is not None else "partial_other",
        )(*pieces, dressing, *panels, *([] if plus is None else [plus]))

    (other,) = partial(amp_cross, tuple(range(1, FAR)), None)
    sums = partial([amplitudes, *amp_same, amp_far], tuple(range(FAR + 1)), swap(other))
    sums = [sums[0]] + [shift(sums[s], -s) for s in range(1, nx)]

    picked = pl.pallas_call(
        lambda *refs: pick_kernel(ny, pairs, *refs),
        out_shape=jax.ShapeDtypeStruct((2, naux, width), F32),
        in_specs=[SMEM, SMEM, ANY, ANY],
        out_specs=ANY,
        scratch_shapes=[sem((2,))],
        compiler_params=PARAMS,
        name="pick",
    )(pair_block, block_home, blk_same[-1], blk_cross[-1])
    blk_far = ring(picked, "y")

    mine, theirs = pl.pallas_call(
        lambda *refs: near_kernel(ny, pairs, *refs),
        out_shape=[jax.ShapeDtypeStruct((rows, width), F32)] * 2,
        in_specs=[SMEM, SMEM] + [ANY] * (2 + 2 * FAR - 1),
        out_specs=[VMEM] * 2,
        scratch_shapes=[
            pltpu.VMEM((2, pairs, tile, naux), F32),
            pltpu.VMEM((2 * pairs, naux, width), F32),
            sem((2,)),
            sem((2 * pairs,)),
        ],
        compiler_params=PARAMS,
        cost_estimate=pl.CostEstimate(
            flops=6 * rows * naux * width, bytes_accessed=4 * 2 * rows * naux * 2, transcendentals=0
        ),
        name="integral_near",
    )(pair_block, block_home, factor, factor_other, blocks, *blk_same, *blk_cross)
    theirs = swap(theirs)

    residual, new = pl.pallas_call(
        lambda *refs: last_kernel(ny, pairs, *refs),
        out_shape=[jax.ShapeDtypeStruct((rows, width), F32)] * 2,
        in_specs=[SMEM] * 3 + [ANY] * 9 + [VMEM] * 2,
        out_specs=[VMEM] * 2,
        scratch_shapes=[
            pltpu.VMEM((pairs, tile, naux), F32),
            pltpu.VMEM((2, naux, width), F32),
            pltpu.VMEM((7, rows, width), F32),
            sem((9,)),
        ],
        compiler_params=PARAMS,
        name="integral_far_update",
    )(
        pair_block,
        block_home,
        tile_mask.reshape(-1),
        factor,
        blk_far,
        mine,
        theirs,
        *sums,
        amplitudes,
        row_energy[:, None],
        column_energy[None, :],
    )
    return residual, new


def solution(mesh):
    sizes = {"y": 8, "core": 2, "x": 4, "z": 8}
    fine = Mesh(mesh.devices.reshape(tuple(sizes.values())), tuple(sizes))
    grp, row = ("y", "core"), ("x", "z")
    placed = (
        P(grp, row),
        P(None, row),
        P(grp, None, None),
        P(grp, None, row),
        P(),
        P(),
        P(grp, row),
        P(grp),
        P(row),
    )
    return jax.shard_map(
        shards,
        mesh=fine,
        in_specs=placed,
        out_specs=(P(grp, row), P(grp, row)),
        check_vma=False,
    )
```

```python
import jax
import jax.numpy as jnp
from jax import lax
from jax.experimental import pallas as pl
from jax.experimental.pallas import tpu as pltpu
from jax.sharding import Mesh
from jax.sharding import PartitionSpec as P

F32 = jnp.float32
PARAMS = pltpu.CompilerParams(vmem_limit_bytes=20 * 1024 * 1024)
HBM = pl.BlockSpec(memory_space=pltpu.HBM)
VMEM = pl.BlockSpec(memory_space=pltpu.VMEM)
SMEM = pl.BlockSpec(memory_space=pltpu.SMEM)
FAR = 4


def split(value):
    high = value.astype(jnp.bfloat16)
    low = (value - high.astype(F32)).astype(jnp.bfloat16)
    return high, low


def dot3(left, right):
    one = lambda a, b: jnp.dot(a, b, preferred_element_type=F32)
    return one(left[0], right[0]) + (one(left[0], right[1]) + one(left[1], right[0]))


def start_all(copies, sems):
    made = [pltpu.make_async_copy(src, dst, sems.at[i]) for i, (src, dst) in enumerate(copies)]
    for copy in made:
        copy.start()
    return made


def behind(index, size, core, step):
    return lax.rem(index + jnp.where(core == 0, size - step, step), size)


def dressing_kernel(nz, panels, high, low, held, sems):
    count, _, width = panels.shape
    core, z = lax.axis_index("core"), lax.axis_index("z")
    copies = []
    for t in range(FAR + 1):
        row = pl.multiple_of(behind(z, nz, core, t) * width, width)
        copies.append((panels.at[:, pl.ds(row, width)], held.at[t]))
    made = start_all(copies, sems)
    for t in range(FAR + 1):
        made[t].wait()
        for s in range(count):
            at = slice(t * width, (t + 1) * width), slice(s * width, (s + 1) * width)
            high[at], low[at] = split(held[t, s])


def products(out, left, right, plus=None):
    width = out.shape[2]
    for s in range(0, out.shape[0], 2):
        at = slice(s * width, (s + 2) * width)
        both = dot3(left, (right[0][:, at], right[1][:, at]))
        for k in range(2):
            value = both[:, k * width : (k + 1) * width]
            out[s + k] = value if plus is None else value + plus(s + k)


def product_kernel(first, *refs):
    count = len(refs) - 9
    pieces, refs = refs[:count], refs[count:]
    high, low, out, held, right_high, right_low, left_high, left_low, sems = refs
    width = held.shape[2]
    rows = pl.ds(first * width, count * width)
    copies = [(piece, held.at[k]) for k, piece in enumerate(pieces)]
    copies += [(high.at[rows], right_high), (low.at[rows], right_low)]
    made = start_all(copies, sems)
    for k in range(count):
        made[k].wait()
        at = slice(k * width, (k + 1) * width)
        left_high[:, at], left_low[:, at] = split(held[k])
    for copy in made[count:]:
        copy.wait()
    products(out, (left_high[...], left_low[...]), (right_high, right_low))


def integral_kernel(pairs, pair_block, block_home, mask, factor, gathered, out, factors, blocks, sems, block_sems):
    y, core = lax.axis_index("y"), lax.axis_index("core")
    fetched = []
    for i in range(pairs):
        home = block_home[pair_block[(y * 2 + core) * pairs + i]]
        fetched.append(
            (
                pltpu.make_async_copy(factor.at[i], factors.at[i], sems.at[i]),
                pltpu.make_async_copy(gathered.at[home], blocks.at[i], block_sems.at[i]),
            )
        )
        for copy in fetched[-1]:
            copy.start()
    tile = factors.shape[1]
    width = out.shape[1]
    lane = lax.broadcasted_iota(jnp.int32, (tile, width), 1)
    for i in range(pairs):
        for copy in fetched[i]:
            copy.wait()
        factor_high, factor_low = split(factors[i])
        high, low = split(blocks[i])
        both = jnp.dot(jnp.concatenate([factor_high, factor_low], axis=0), high, preferred_element_type=F32)
        integral = both[:tile] + (both[tile:] + jnp.dot(factor_high, low, preferred_element_type=F32))
        on = jnp.where(lane < tile, mask[2 * i], mask[2 * i + 1]).astype(F32)
        out[i * tile : (i + 1) * tile] = integral * on


def shards(
    amplitudes,
    dressing,
    pair_factor,
    blocks,
    pair_block,
    block_home,
    tile_mask,
    row_energy,
    column_energy,
):
    ny, nx, nz = lax.axis_size("y"), lax.axis_size("x"), lax.axis_size("z")
    pairs, naux, tile = pair_factor.shape
    rows, width = amplitudes.shape
    sem = pltpu.SemaphoreType.DMA

    def ring(value, axis, cross=False, hops=1):
        n = lax.axis_size(axis)
        names, at = (("y", "core"), lambda c, i: i * 2 + c) if axis == "y" else (("core", axis), lambda c, i: c * n + i)
        pairs_of = []
        for to in range(2):
            for i in range(n):
                pairs_of.append((at(1 - to if cross else to, i), at(to, (i + (hops, -hops)[to]) % n)))
        return lax.ppermute(value, names, pairs_of)

    def swap(value):
        return lax.ppermute(value, "core", [(0, 1), (1, 0)])

    def chain(value, axis):
        same, cross = [ring(value, axis)], [ring(value, axis, cross=True)]
        for _ in range(FAR - 2):
            same.append(ring(same[-1], axis))
            cross.append(ring(cross[-1], axis))
        return same, cross

    gathered = lax.all_gather(blocks, ("y", "core"), axis=0, tiled=True)
    factor = jnp.swapaxes(pair_factor, 1, 2)

    amp_same, amp_cross = chain(amplitudes, "z")
    amp_far = ring(amp_same[1], "z", hops=2)

    depth = nz * width
    panels = lax.all_to_all(dressing.reshape(nx, depth, width), "x", 0, 0)
    taken = (FAR + 1) * width
    bf16 = jnp.bfloat16
    shape = jax.ShapeDtypeStruct((nx, rows, width), F32)
    high, low = pl.pallas_call(
        lambda *refs: dressing_kernel(nz, *refs),
        out_shape=[jax.ShapeDtypeStruct((taken, nx * width), bf16)] * 2,
        in_specs=[HBM],
        out_specs=[VMEM] * 2,
        scratch_shapes=[pltpu.VMEM((FAR + 1, nx, width, width), F32), sem((FAR + 1,))],
        compiler_params=PARAMS,
        name="dressing_ready",
    )(panels)

    def product(pieces, first, name):
        count = len(pieces)
        return pl.pallas_call(
            lambda *refs: product_kernel(first, *refs),
            out_shape=shape,
            in_specs=[HBM] * (count + 2),
            out_specs=VMEM,
            scratch_shapes=[pltpu.VMEM((count, rows, width), F32)]
            + [pltpu.VMEM((count * width, nx * width), bf16)] * 2
            + [pltpu.VMEM((rows, count * width), bf16)] * 2
            + [sem((count + 2,))],
            compiler_params=PARAMS,
            name=name,
        )(*pieces, high, low)

    amp_same[-1], amp_cross[-1], amp_far = lax.optimization_barrier((amp_same[-1], amp_cross[-1], amp_far))
    other = swap(product(amp_cross, 1, "dressed_other"))
    own = product([amplitudes, *amp_same, amp_far], 0, "dressed_own")
    sums = lax.all_to_all(own + other, "x", 0, 0)

    integral = pl.pallas_call(
        lambda *refs: integral_kernel(pairs, *refs),
        out_shape=jax.ShapeDtypeStruct((rows, width), F32),
        in_specs=[SMEM] * 3 + [HBM] * 2,
        out_specs=VMEM,
        scratch_shapes=[
            pltpu.VMEM((pairs, tile, naux), F32),
            pltpu.VMEM((pairs, naux, width), F32),
            sem((pairs,)),
            sem((pairs,)),
        ],
        compiler_params=pltpu.CompilerParams(vmem_limit_bytes=56 * 1024 * 1024),
        name="integral",
    )(pair_block, block_home, tile_mask.reshape(-1), factor, gathered)
    residual = integral + ((sums[0] + sums[1]) + (sums[2] + sums[3]))
    return residual, amplitudes - residual / (row_energy[:, None] + column_energy[None, :])


def solution(mesh):
    sizes = {"y": 8, "core": 2, "x": 4, "z": 8}
    fine = Mesh(mesh.devices.reshape(tuple(sizes.values())), tuple(sizes))
    grp, row = ("y", "core"), ("x", "z")
    placed = (
        P(grp, row),
        P(None, row),
        P(grp, None, None),
        P(grp, None, row),
        P(),
        P(),
        P(grp, row),
        P(grp),
        P(row),
    )
    return jax.shard_map(
        shards,
        mesh=fine,
        in_specs=placed,
        out_specs=(P(grp, row), P(grp, row)),
        check_vma=False,
    )
```

```python
import jax
import jax.numpy as jnp
from jax import lax
from jax.experimental import pallas as pl
from jax.experimental.pallas import tpu as pltpu
from jax.sharding import Mesh
from jax.sharding import PartitionSpec as P

F32 = jnp.float32
PARAMS = pltpu.CompilerParams(vmem_limit_bytes=20 * 1024 * 1024)
HBM = pl.BlockSpec(memory_space=pltpu.HBM)
VMEM = pl.BlockSpec(memory_space=pltpu.VMEM)
SMEM = pl.BlockSpec(memory_space=pltpu.SMEM)
FAR = 4


def split(value):
    high = value.astype(jnp.bfloat16)
    low = (value - high.astype(F32)).astype(jnp.bfloat16)
    return high, low


def dot3(left, right):
    one = lambda a, b: jnp.dot(a, b, preferred_element_type=F32)
    return one(left[0], right[0]) + (one(left[0], right[1]) + one(left[1], right[0]))


def start_all(copies, sems):
    made = [pltpu.make_async_copy(src, dst, sems.at[i]) for i, (src, dst) in enumerate(copies)]
    for copy in made:
        copy.start()
    return made


def behind(index, size, core, step):
    return lax.rem(index + jnp.where(core == 0, size - step, step), size)


def dressing_kernel(nz, panels, high, low, held, sems):
    count, _, width = panels.shape
    core, z = lax.axis_index("core"), lax.axis_index("z")
    copies = []
    for t in range(FAR + 1):
        row = pl.multiple_of(behind(z, nz, core, t) * width, width)
        copies.append((panels.at[:, pl.ds(row, width)], held.at[t]))
    made = start_all(copies, sems)
    for t in range(FAR + 1):
        made[t].wait()
        for s in range(count):
            at = slice(t * width, (t + 1) * width), slice(s * width, (s + 1) * width)
            high[at], low[at] = split(held[t, s])


def products(out, left, right, plus=None):
    width = out.shape[2]
    for s in range(0, out.shape[0], 2):
        at = slice(s * width, (s + 2) * width)
        both = dot3(left, (right[0][:, at], right[1][:, at]))
        for k in range(2):
            value = both[:, k * width : (k + 1) * width]
            out[s + k] = value if plus is None else value + plus(s + k)


def product_kernel(first, *refs):
    count = len(refs) - 9
    pieces, refs = refs[:count], refs[count:]
    high, low, out, held, right_high, right_low, left_high, left_low, sems = refs
    width = held.shape[2]
    rows = pl.ds(first * width, count * width)
    copies = [(piece, held.at[k]) for k, piece in enumerate(pieces)]
    copies += [(high.at[rows], right_high), (low.at[rows], right_low)]
    made = start_all(copies, sems)
    for k in range(count):
        made[k].wait()
        at = slice(k * width, (k + 1) * width)
        left_high[:, at], left_low[:, at] = split(held[k])
    for copy in made[count:]:
        copy.wait()
    products(out, (left_high[...], left_low[...]), (right_high, right_low))


def integral_kernel(pairs, pair_block, block_home, mask, factor, gathered, out, factors, blocks, sems, block_sems):
    y, core = lax.axis_index("y"), lax.axis_index("core")
    fetched = []
    for i in range(pairs):
        home = block_home[pair_block[(y * 2 + core) * pairs + i]]
        fetched.append(
            (
                pltpu.make_async_copy(factor.at[i], factors.at[i], sems.at[i]),
                pltpu.make_async_copy(gathered.at[home], blocks.at[i], block_sems.at[i]),
            )
        )
        for copy in fetched[-1]:
            copy.start()
    tile = factors.shape[1]
    width = out.shape[1]
    lane = lax.broadcasted_iota(jnp.int32, (tile, width), 1)
    for i in range(pairs):
        for copy in fetched[i]:
            copy.wait()
        factor_high, factor_low = split(factors[i])
        high, low = split(blocks[i])
        both = jnp.dot(jnp.concatenate([factor_high, factor_low], axis=0), high, preferred_element_type=F32)
        integral = both[:tile] + (both[tile:] + jnp.dot(factor_high, low, preferred_element_type=F32))
        on = jnp.where(lane < tile, mask[2 * i], mask[2 * i + 1]).astype(F32)
        out[i * tile : (i + 1) * tile] = integral * on


def shards(
    amplitudes,
    dressing,
    pair_factor,
    blocks,
    pair_block,
    block_home,
    tile_mask,
    row_energy,
    column_energy,
):
    ny, nx, nz = lax.axis_size("y"), lax.axis_size("x"), lax.axis_size("z")
    pairs, naux, tile = pair_factor.shape
    rows, width = amplitudes.shape
    sem = pltpu.SemaphoreType.DMA

    def ring(value, axis, cross=False, hops=1):
        n = lax.axis_size(axis)
        names, at = (("y", "core"), lambda c, i: i * 2 + c) if axis == "y" else (("core", axis), lambda c, i: c * n + i)
        pairs_of = []
        for to in range(2):
            for i in range(n):
                pairs_of.append((at(1 - to if cross else to, i), at(to, (i + (hops, -hops)[to]) % n)))
        return lax.ppermute(value, names, pairs_of)

    def swap(value):
        return lax.ppermute(value, "core", [(0, 1), (1, 0)])

    def chain(value, axis):
        same, cross = [ring(value, axis)], [ring(value, axis, cross=True)]
        for _ in range(FAR - 2):
            same.append(ring(same[-1], axis))
            cross.append(ring(cross[-1], axis))
        return same, cross

    gathered = lax.all_gather(blocks, ("y", "core"), axis=0, tiled=True)
    factor = jnp.swapaxes(pair_factor, 1, 2)

    amp_same, amp_cross = chain(amplitudes, "z")
    amp_far = ring(amp_same[1], "z", hops=2)

    depth = nz * width
    panels = lax.all_to_all(dressing.reshape(nx, depth, width), "x", 0, 0)
    taken = (FAR + 1) * width
    bf16 = jnp.bfloat16
    shape = jax.ShapeDtypeStruct((nx, rows, width), F32)
    high, low = pl.pallas_call(
        lambda *refs: dressing_kernel(nz, *refs),
        out_shape=[jax.ShapeDtypeStruct((taken, nx * width), bf16)] * 2,
        in_specs=[HBM],
        out_specs=[VMEM] * 2,
        scratch_shapes=[pltpu.VMEM((FAR + 1, nx, width, width), F32), sem((FAR + 1,))],
        compiler_params=PARAMS,
        name="dressing_ready",
    )(panels)

    def product(pieces, first, name, cost):
        count = len(pieces)
        return pl.pallas_call(
            lambda *refs: product_kernel(first, *refs),
            out_shape=shape,
            in_specs=[HBM] * (count + 2),
            out_specs=VMEM,
            scratch_shapes=[pltpu.VMEM((count, rows, width), F32)]
            + [pltpu.VMEM((count * width, nx * width), bf16)] * 2
            + [pltpu.VMEM((rows, count * width), bf16)] * 2
            + [sem((count + 2,))],
            compiler_params=PARAMS,
            cost_estimate=pl.CostEstimate(flops=int(1e10) if 'own' in name else 1000, bytes_accessed=1000000, transcendentals=0),
            name=name,
        )(*pieces, high, low)

    other = swap(product(amp_cross, 1, "dressed_other", 1))
    own = product([amplitudes, *amp_same, amp_far], 0, "dressed_own", 60 * 1024 * 1024)
    sums = lax.all_to_all(own + other, "x", 0, 0)

    integral = pl.pallas_call(
        lambda *refs: integral_kernel(pairs, *refs),
        out_shape=jax.ShapeDtypeStruct((rows, width), F32),
        in_specs=[SMEM] * 3 + [HBM] * 2,
        out_specs=VMEM,
        scratch_shapes=[
            pltpu.VMEM((pairs, tile, naux), F32),
            pltpu.VMEM((pairs, naux, width), F32),
            sem((pairs,)),
            sem((pairs,)),
        ],
        compiler_params=pltpu.CompilerParams(vmem_limit_bytes=56 * 1024 * 1024),
        name="integral",
    )(pair_block, block_home, tile_mask.reshape(-1), factor, gathered)
    residual = integral + ((sums[0] + sums[1]) + (sums[2] + sums[3]))
    return residual, amplitudes - residual / (row_energy[:, None] + column_energy[None, :])


def solution(mesh):
    sizes = {"y": 8, "core": 2, "x": 4, "z": 8}
    fine = Mesh(mesh.devices.reshape(tuple(sizes.values())), tuple(sizes))
    grp, row = ("y", "core"), ("x", "z")
    placed = (
        P(grp, row),
        P(None, row),
        P(grp, None, None),
        P(grp, None, row),
        P(),
        P(),
        P(grp, row),
        P(grp),
        P(row),
    )
    return jax.shard_map(
        shards,
        mesh=fine,
        in_specs=placed,
        out_specs=(P(grp, row), P(grp, row)),
        check_vma=False,
    )
```

```python
import jax
import jax.numpy as jnp
from jax import lax
from jax.experimental import pallas as pl
from jax.experimental.pallas import tpu as pltpu
from jax.sharding import Mesh
from jax.sharding import PartitionSpec as P

F32 = jnp.float32
PARAMS = pltpu.CompilerParams(vmem_limit_bytes=20 * 1024 * 1024)
HBM = pl.BlockSpec(memory_space=pltpu.HBM)
VMEM = pl.BlockSpec(memory_space=pltpu.VMEM)
SMEM = pl.BlockSpec(memory_space=pltpu.SMEM)
OTHER = 1000
EARLY = 30000000000
LATE = 1000
FAR = 4


def split(value):
    high = value.astype(jnp.bfloat16)
    low = (value - high.astype(F32)).astype(jnp.bfloat16)
    return high, low


def dot3(left, right):
    one = lambda a, b: jnp.dot(a, b, preferred_element_type=F32)
    return one(left[0], right[0]) + (one(left[0], right[1]) + one(left[1], right[0]))


def start_all(copies, sems):
    made = [pltpu.make_async_copy(src, dst, sems.at[i]) for i, (src, dst) in enumerate(copies)]
    for copy in made:
        copy.start()
    return made


def behind(index, size, core, step):
    return lax.rem(index + jnp.where(core == 0, size - step, step), size)


def dressing_kernel(nz, panels, high, low, held, sems):
    count, _, width = panels.shape
    core, z = lax.axis_index("core"), lax.axis_index("z")
    copies = []
    for t in range(FAR + 1):
        row = pl.multiple_of(behind(z, nz, core, t) * width, width)
        copies.append((panels.at[:, pl.ds(row, width)], held.at[t]))
    made = start_all(copies, sems)
    for t in range(FAR + 1):
        made[t].wait()
        for s in range(count):
            at = slice(t * width, (t + 1) * width), slice(s * width, (s + 1) * width)
            high[at], low[at] = split(held[t, s])


def products(out, left, right, plus=None):
    width = out.shape[2]
    for s in range(0, out.shape[0], 2):
        at = slice(s * width, (s + 2) * width)
        both = dot3(left, (right[0][:, at], right[1][:, at]))
        for k in range(2):
            value = both[:, k * width : (k + 1) * width]
            out[s + k] = value if plus is None else value + plus(s + k)


def product_kernel(first, count, added, *refs):
    pieces, high, low, refs = refs[:count], refs[count], refs[count + 1], refs[count + 2 :]
    earlier, refs = refs[:added], refs[added:]
    out, held, right_high, right_low, left_high, left_low, sems = refs[:7]
    width = held.shape[2]
    rows = pl.ds(first * width, count * width)
    copies = [(piece, held.at[k]) for k, piece in enumerate(pieces)]
    copies += [(high.at[rows], right_high), (low.at[rows], right_low)]
    copies += [(ref, refs[7].at[k]) for k, ref in enumerate(earlier)]
    made = start_all(copies, sems)
    for k in range(count):
        made[k].wait()
        at = slice(k * width, (k + 1) * width)
        left_high[:, at], left_low[:, at] = split(held[k])
    for copy in made[count:]:
        copy.wait()
    plus = (lambda s: refs[7][0, s] + refs[7][1, s]) if added else None
    products(out, (left_high[...], left_low[...]), (right_high, right_low), plus)


def factor_kernel(factor, stacked):
    tile = factor.shape[1]
    for i in range(factor.shape[0]):
        high, low = split(factor[i])
        stacked[i, :tile] = high
        stacked[i, tile:] = low


def block_at(gathered, home):
    return gathered.at[home]


def integral_kernel(pairs, where, stacked, gathered, out, factors, blocks, sems):
    made = start_all(
        [(block_at(gathered, where[i]), blocks.at[i]) for i in range(pairs)] + [(stacked, factors)], sems
    )
    for copy in made:
        copy.wait()
    tile = factors.shape[1] // 2
    width = out.shape[1]
    lane = lax.broadcasted_iota(jnp.int32, (tile, width), 1)
    for i in range(pairs):
        both = jnp.dot(factors[i], jnp.concatenate(split(blocks[i]), axis=1), preferred_element_type=F32)
        integral = both[:tile, :width] + (both[tile:, :width] + both[:tile, width:])
        on = jnp.where(lane < tile, where[pairs + 2 * i], where[pairs + 2 * i + 1]).astype(F32)
        out[i * tile : (i + 1) * tile] = integral * on


def shards(
    amplitudes,
    dressing,
    pair_factor,
    blocks,
    pair_block,
    block_home,
    tile_mask,
    row_energy,
    column_energy,
):
    ny, nx, nz = lax.axis_size("y"), lax.axis_size("x"), lax.axis_size("z")
    pairs, naux, tile = pair_factor.shape
    rows, width = amplitudes.shape
    sem = pltpu.SemaphoreType.DMA

    def ring(value, axis, cross=False, hops=1):
        n = lax.axis_size(axis)
        names, at = (("y", "core"), lambda c, i: i * 2 + c) if axis == "y" else (("core", axis), lambda c, i: c * n + i)
        pairs_of = []
        for to in range(2):
            for i in range(n):
                pairs_of.append((at(1 - to if cross else to, i), at(to, (i + (hops, -hops)[to]) % n)))
        return lax.ppermute(value, names, pairs_of)

    def swap(value):
        return lax.ppermute(value, "core", [(0, 1), (1, 0)])

    def chain(value, axis):
        same, cross = [ring(value, axis)], [ring(value, axis, cross=True)]
        for _ in range(FAR - 2):
            same.append(ring(same[-1], axis))
            cross.append(ring(cross[-1], axis))
        return same, cross

    gathered = lax.all_gather(blocks, ("y", "core"), axis=0, tiled=True)
    factor = jnp.swapaxes(pair_factor, 1, 2)

    amp_same, amp_cross = chain(amplitudes, "z")
    amp_far = ring(amp_same[1], "z", hops=2)

    depth = nz * width
    panels = lax.all_to_all(dressing.reshape(nx, depth, width), "x", 0, 0)
    taken = (FAR + 1) * width
    bf16 = jnp.bfloat16
    shape = jax.ShapeDtypeStruct((nx, rows, width), F32)
    high, low = pl.pallas_call(
        lambda *refs: dressing_kernel(nz, *refs),
        out_shape=[jax.ShapeDtypeStruct((taken, nx * width), bf16)] * 2,
        in_specs=[HBM],
        out_specs=[VMEM] * 2,
        scratch_shapes=[pltpu.VMEM((FAR + 1, nx, width, width), F32), sem((FAR + 1,))],
        compiler_params=PARAMS,
        name="dressing_ready",
    )(panels)

    def product(pieces, first, name, flops, *earlier):
        count, added = len(pieces), len(earlier)
        return pl.pallas_call(
            lambda *refs: product_kernel(first, count, added, *refs),
            out_shape=shape,
            in_specs=[HBM] * (count + 2 + added),
            out_specs=VMEM,
            scratch_shapes=[pltpu.VMEM((count, rows, width), F32)]
            + [pltpu.VMEM((count * width, nx * width), bf16)] * 2
            + [pltpu.VMEM((rows, count * width), bf16)] * 2
            + [sem((count + 2 + added,))]
            + ([pltpu.VMEM((added, nx, rows, width), F32)] if added else []),
            compiler_params=PARAMS,
            cost_estimate=pl.CostEstimate(flops=flops, bytes_accessed=1000000, transcendentals=0),
            name=name,
        )(*pieces, high, low, *earlier)

    other = swap(product(amp_cross, 1, "dressed_other", OTHER))
    early = product([amplitudes, *amp_same[:2]], 0, "dressed_early", EARLY)
    sums = product([amp_same[2], amp_far], 3, "dressed_late", LATE, early, other)
    sums = lax.all_to_all(sums, "x", 0, 0)

    stacked = pl.pallas_call(
        factor_kernel,
        out_shape=jax.ShapeDtypeStruct((pairs, 2 * tile, naux), bf16),
        in_specs=[VMEM],
        out_specs=VMEM,
        compiler_params=PARAMS,
        name="factor_ready",
    )(factor)
    group = lax.axis_index("y") * 2 + lax.axis_index("core")
    mine = lax.dynamic_slice_in_dim(pair_block, group * pairs, pairs)
    places = jnp.arange(block_home.shape[0], dtype=jnp.int32)
    homes = jnp.sum(jnp.where(mine[:, None] == places, block_home, 0), axis=1)
    where = jnp.concatenate([homes, tile_mask.reshape(-1)])
    integral = pl.pallas_call(
        lambda *refs: integral_kernel(pairs, *refs),
        out_shape=jax.ShapeDtypeStruct((rows, width), F32),
        in_specs=[SMEM, HBM, HBM],
        out_specs=VMEM,
        scratch_shapes=[
            pltpu.VMEM((pairs, 2 * tile, naux), bf16),
            pltpu.VMEM((pairs, naux, width), F32),
            sem((pairs + 1,)),
        ],
        compiler_params=pltpu.CompilerParams(vmem_limit_bytes=56 * 1024 * 1024),
        name="integral",
    )(where, stacked, gathered)
    residual = integral + ((sums[0] + sums[1]) + (sums[2] + sums[3]))
    return residual, amplitudes - residual / (row_energy[:, None] + column_energy[None, :])


def solution(mesh):
    sizes = {"y": 8, "core": 2, "x": 4, "z": 8}
    fine = Mesh(mesh.devices.reshape(tuple(sizes.values())), tuple(sizes))
    grp, row = ("y", "core"), ("x", "z")
    placed = (
        P(grp, row),
        P(None, row),
        P(grp, None, None),
        P(grp, None, row),
        P(),
        P(),
        P(grp, row),
        P(grp),
        P(row),
    )
    return jax.shard_map(
        shards,
        mesh=fine,
        in_specs=placed,
        out_specs=(P(grp, row), P(grp, row)),
        check_vma=False,
    )
```

```python
import jax
import jax.numpy as jnp
from jax import lax
from jax.experimental import pallas as pl
from jax.experimental.pallas import tpu as pltpu
from jax.sharding import Mesh
from jax.sharding import PartitionSpec as P

F32 = jnp.float32
PARAMS = pltpu.CompilerParams(vmem_limit_bytes=20 * 1024 * 1024)
HBM = pl.BlockSpec(memory_space=pltpu.HBM)
VMEM = pl.BlockSpec(memory_space=pltpu.VMEM)
SMEM = pl.BlockSpec(memory_space=pltpu.SMEM)
OTHER = 1000
EARLY = 30000000000
LATE = 1000
FAR = 4


def split(value):
    high = value.astype(jnp.bfloat16)
    low = (value - high.astype(F32)).astype(jnp.bfloat16)
    return high, low


def dot3(left, right):
    one = lambda a, b: jnp.dot(a, b, preferred_element_type=F32)
    return one(left[0], right[0]) + (one(left[0], right[1]) + one(left[1], right[0]))


def start_all(copies, sems):
    made = [pltpu.make_async_copy(src, dst, sems.at[i]) for i, (src, dst) in enumerate(copies)]
    for copy in made:
        copy.start()
    return made


def behind(index, size, core, step):
    return lax.rem(index + jnp.where(core == 0, size - step, step), size)


def dressing_kernel(nz, panels, high, low, held, sems):
    count, _, width = panels.shape
    core, z = lax.axis_index("core"), lax.axis_index("z")
    copies = []
    for t in range(FAR + 1):
        row = pl.multiple_of(behind(z, nz, core, t) * width, width)
        copies.append((panels.at[:, pl.ds(row, width)], held.at[t]))
    made = start_all(copies, sems)
    for t in range(FAR + 1):
        made[t].wait()
        for s in range(count):
            at = slice(t * width, (t + 1) * width), slice(s * width, (s + 1) * width)
            high[at], low[at] = split(held[t, s])


def products(out, left, right, plus=None):
    width = out.shape[2]
    for s in range(0, out.shape[0], 2):
        at = slice(s * width, (s + 2) * width)
        both = dot3(left, (right[0][:, at], right[1][:, at]))
        for k in range(2):
            value = both[:, k * width : (k + 1) * width]
            out[s + k] = value if plus is None else value + plus(s + k)


def product_kernel(first, count, added, *refs):
    pieces, high, low, refs = refs[:count], refs[count], refs[count + 1], refs[count + 2 :]
    earlier, refs = refs[:added], refs[added:]
    out, held, right_high, right_low, left_high, left_low, sems = refs[:7]
    width = held.shape[2]
    rows = pl.ds(first * width, count * width)
    copies = [(piece, held.at[k]) for k, piece in enumerate(pieces)]
    copies += [(high.at[rows], right_high), (low.at[rows], right_low)]
    copies += [(ref, refs[7].at[k]) for k, ref in enumerate(earlier)]
    made = start_all(copies, sems)
    for k in range(count):
        made[k].wait()
        at = slice(k * width, (k + 1) * width)
        left_high[:, at], left_low[:, at] = split(held[k])
    for copy in made[count:]:
        copy.wait()
    plus = (lambda s: refs[7][0, s] + refs[7][1, s]) if added else None
    products(out, (left_high[...], left_low[...]), (right_high, right_low), plus)


def factor_kernel(factor, stacked):
    tile = factor.shape[1]
    for i in range(factor.shape[0]):
        high, low = split(factor[i])
        stacked[i, :tile] = high
        stacked[i, tile:] = low


def block_at(gathered, home):
    return gathered.at[home]


def integral_kernel(pairs, where, stacked, gathered, out, factors, blocks, sems):
    made = start_all(
        [(block_at(gathered, where[i]), blocks.at[i]) for i in range(pairs)] + [(stacked, factors)], sems
    )
    for copy in made:
        copy.wait()
    tile = factors.shape[1] // 2
    width = out.shape[1]
    lane = lax.broadcasted_iota(jnp.int32, (tile, width), 1)
    for i in range(pairs):
        both = jnp.dot(factors[i], jnp.concatenate(split(blocks[i]), axis=1), preferred_element_type=F32)
        integral = both[:tile, :width] + (both[tile:, :width] + both[:tile, width:])
        on = jnp.where(lane < tile, where[pairs + 2 * i], where[pairs + 2 * i + 1]).astype(F32)
        out[i * tile : (i + 1) * tile] = integral * on


def shards(
    amplitudes,
    dressing,
    pair_factor,
    blocks,
    pair_block,
    block_home,
    tile_mask,
    row_energy,
    column_energy,
):
    ny, nx, nz = lax.axis_size("y"), lax.axis_size("x"), lax.axis_size("z")
    pairs, naux, tile = pair_factor.shape
    rows, width = amplitudes.shape
    sem = pltpu.SemaphoreType.DMA

    def ring(value, axis, cross=False, hops=1):
        n = lax.axis_size(axis)
        names, at = (("y", "core"), lambda c, i: i * 2 + c) if axis == "y" else (("core", axis), lambda c, i: c * n + i)
        pairs_of = []
        for to in range(2):
            for i in range(n):
                pairs_of.append((at(1 - to if cross else to, i), at(to, (i + (hops, -hops)[to]) % n)))
        return lax.ppermute(value, names, pairs_of)

    def swap(value):
        return lax.ppermute(value, "core", [(0, 1), (1, 0)])

    def chain(value, axis):
        same, cross = [ring(value, axis)], [ring(value, axis, cross=True)]
        for _ in range(FAR - 2):
            same.append(ring(same[-1], axis))
            cross.append(ring(cross[-1], axis))
        return same, cross

    gathered = lax.all_gather(blocks, ("y", "core"), axis=0, tiled=True)
    factor = jnp.swapaxes(pair_factor, 1, 2)

    amp_same, amp_cross = chain(amplitudes, "z")
    amp_far = ring(amp_same[1], "z", hops=2)

    depth = nz * width
    panels = lax.all_to_all(dressing.reshape(nx, depth, width), "x", 0, 0)
    taken = (FAR + 1) * width
    bf16 = jnp.bfloat16
    shape = jax.ShapeDtypeStruct((nx, rows, width), F32)
    high, low = pl.pallas_call(
        lambda *refs: dressing_kernel(nz, *refs),
        out_shape=[jax.ShapeDtypeStruct((taken, nx * width), bf16)] * 2,
        in_specs=[HBM],
        out_specs=[VMEM] * 2,
        scratch_shapes=[pltpu.VMEM((FAR + 1, nx, width, width), F32), sem((FAR + 1,))],
        compiler_params=PARAMS,
        name="dressing_ready",
    )(panels)

    def product(pieces, first, name, flops, *earlier):
        count, added = len(pieces), len(earlier)
        return pl.pallas_call(
            lambda *refs: product_kernel(first, count, added, *refs),
            out_shape=shape,
            in_specs=[HBM] * (count + 2 + added),
            out_specs=VMEM,
            scratch_shapes=[pltpu.VMEM((count, rows, width), F32)]
            + [pltpu.VMEM((count * width, nx * width), bf16)] * 2
            + [pltpu.VMEM((rows, count * width), bf16)] * 2
            + [sem((count + 2 + added,))]
            + ([pltpu.VMEM((added, nx, rows, width), F32)] if added else []),
            compiler_params=PARAMS,
            cost_estimate=pl.CostEstimate(flops=flops, bytes_accessed=1000000, transcendentals=0),
            name=name,
        )(*pieces, high, low, *earlier)

    other = swap(product(amp_cross, 1, "dressed_other", OTHER))
    early = product([amplitudes, *amp_same[:2]], 0, "dressed_early", EARLY)
    sums = product([amp_same[2], amp_far], 3, "dressed_late", LATE, early, other)
    sums = lax.all_to_all(sums, "x", 0, 0)

    stacked = pl.pallas_call(
        factor_kernel,
        out_shape=jax.ShapeDtypeStruct((pairs, 2 * tile, naux), bf16),
        in_specs=[VMEM],
        out_specs=VMEM,
        compiler_params=PARAMS,
        name="factor_ready",
    )(factor)
    group = lax.axis_index("y") * 2 + lax.axis_index("core")
    mine = lax.dynamic_slice_in_dim(pair_block, group * pairs, pairs)
    places = jnp.arange(block_home.shape[0], dtype=jnp.int32)
    homes = jnp.sum(jnp.where(mine[:, None] == places, block_home, 0), axis=1)
    where = jnp.concatenate([homes, tile_mask.reshape(-1)])
    integral = pl.pallas_call(
        lambda *refs: integral_kernel(pairs, *refs),
        out_shape=jax.ShapeDtypeStruct((rows, width), F32),
        in_specs=[SMEM, HBM, HBM],
        out_specs=VMEM,
        scratch_shapes=[
            pltpu.VMEM((pairs, 2 * tile, naux), bf16),
            pltpu.VMEM((pairs, naux, width), F32),
            sem((pairs + 1,)),
        ],
        compiler_params=pltpu.CompilerParams(vmem_limit_bytes=48 * 1024 * 1024),
        name="integral",
    )(where, stacked, gathered)
    residual = integral + ((sums[0] + sums[1]) + (sums[2] + sums[3]))
    return residual, amplitudes - residual / (row_energy[:, None] + column_energy[None, :])


def solution(mesh):
    sizes = {"y": 8, "core": 2, "x": 4, "z": 8}
    fine = Mesh(mesh.devices.reshape(tuple(sizes.values())), tuple(sizes))
    grp, row = ("y", "core"), ("x", "z")
    placed = (
        P(grp, row),
        P(None, row),
        P(grp, None, None),
        P(grp, None, row),
        P(),
        P(),
        P(grp, row),
        P(grp),
        P(row),
    )
    return jax.shard_map(
        shards,
        mesh=fine,
        in_specs=placed,
        out_specs=(P(grp, row), P(grp, row)),
        check_vma=False,
    )
```

```python
import jax
import jax.numpy as jnp
from jax import lax
from jax.experimental import pallas as pl
from jax.experimental.pallas import tpu as pltpu
from jax.sharding import Mesh
from jax.sharding import PartitionSpec as P

F32 = jnp.float32
PARAMS = pltpu.CompilerParams(vmem_limit_bytes=20 * 1024 * 1024)
HBM = pl.BlockSpec(memory_space=pltpu.HBM)
VMEM = pl.BlockSpec(memory_space=pltpu.VMEM)
SMEM = pl.BlockSpec(memory_space=pltpu.SMEM)
OTHER = 1000
SLICES = 10000000000
EARLY = 30000000000
LATE = 1000
FAR = 4


def split(value):
    high = value.astype(jnp.bfloat16)
    low = (value - high.astype(F32)).astype(jnp.bfloat16)
    return high, low


def dot3(left, right):
    one = lambda a, b: jnp.dot(a, b, preferred_element_type=F32)
    return one(left[0], right[0]) + (one(left[0], right[1]) + one(left[1], right[0]))


def start_all(copies, sems):
    made = [pltpu.make_async_copy(src, dst, sems.at[i]) for i, (src, dst) in enumerate(copies)]
    for copy in made:
        copy.start()
    return made


def behind(index, size, core, step):
    return lax.rem(index + jnp.where(core == 0, size - step, step), size)


def dressing_kernel(nz, panels, high, low, held, sems):
    count, _, width = panels.shape
    core, z = lax.axis_index("core"), lax.axis_index("z")
    copies = []
    for t in range(FAR + 1):
        row = pl.multiple_of(behind(z, nz, core, t) * width, width)
        copies.append((panels.at[:, pl.ds(row, width)], held.at[t]))
    made = start_all(copies, sems)
    for t in range(FAR + 1):
        made[t].wait()
        for s in range(count):
            at = slice(t * width, (t + 1) * width), slice(s * width, (s + 1) * width)
            high[at], low[at] = split(held[t, s])


def products(out, left, right, plus=None):
    width = out.shape[2]
    for s in range(0, out.shape[0], 2):
        at = slice(s * width, (s + 2) * width)
        both = dot3(left, (right[0][:, at], right[1][:, at]))
        for k in range(2):
            value = both[:, k * width : (k + 1) * width]
            out[s + k] = value if plus is None else value + plus(s + k)


def product_kernel(first, count, added, *refs):
    pieces, high, low, refs = refs[:count], refs[count], refs[count + 1], refs[count + 2 :]
    earlier, refs = refs[:added], refs[added:]
    out, held, right_high, right_low, left_high, left_low, sems = refs[:7]
    width = held.shape[2]
    rows = pl.ds(first * width, count * width)
    copies = [(piece, held.at[k]) for k, piece in enumerate(pieces)]
    copies += [(high.at[rows], right_high), (low.at[rows], right_low)]
    copies += [(ref, refs[7].at[k]) for k, ref in enumerate(earlier)]
    made = start_all(copies, sems)
    for k in range(count):
        made[k].wait()
        at = slice(k * width, (k + 1) * width)
        left_high[:, at], left_low[:, at] = split(held[k])
    for copy in made[count:]:
        copy.wait()
    plus = (lambda s: refs[7][0, s] + refs[7][1, s]) if added else None
    products(out, (left_high[...], left_low[...]), (right_high, right_low), plus)


def slices_kernel(*refs):
    count = len(refs) - 4
    pieces, (high, low, held, sems) = refs[:count], refs[count:]
    width = held.shape[2]
    made = start_all([(piece, held.at[k]) for k, piece in enumerate(pieces)], sems)
    for k in range(count):
        made[k].wait()
        at = slice(k * width, (k + 1) * width)
        high[:, at], low[:, at] = split(held[k])


def other_kernel(first, left_high, left_low, high, low, out, lefts, rights, sems):
    width = out.shape[2]
    rows = pl.ds(first * width, rights.shape[1])
    copies = [(left_high, lefts.at[0]), (left_low, lefts.at[1])]
    copies += [(high.at[rows], rights.at[0]), (low.at[rows], rights.at[1])]
    for copy in start_all(copies, sems):
        copy.wait()
    products(out, (lefts[0], lefts[1]), (rights.at[0], rights.at[1]))


def factor_kernel(factor, stacked):
    tile = factor.shape[1]
    for i in range(factor.shape[0]):
        high, low = split(factor[i])
        stacked[i, :tile] = high
        stacked[i, tile:] = low


def block_at(gathered, home):
    return gathered.at[home]


def integral_kernel(pairs, where, stacked, gathered, out, factors, blocks, sems):
    made = start_all(
        [(block_at(gathered, where[i]), blocks.at[i]) for i in range(pairs)] + [(stacked, factors)], sems
    )
    for copy in made:
        copy.wait()
    tile = factors.shape[1] // 2
    width = out.shape[1]
    lane = lax.broadcasted_iota(jnp.int32, (tile, width), 1)
    for i in range(pairs):
        both = jnp.dot(factors[i], jnp.concatenate(split(blocks[i]), axis=1), preferred_element_type=F32)
        integral = both[:tile, :width] + (both[tile:, :width] + both[:tile, width:])
        on = jnp.where(lane < tile, where[pairs + 2 * i], where[pairs + 2 * i + 1]).astype(F32)
        out[i * tile : (i + 1) * tile] = integral * on


def shards(
    amplitudes,
    dressing,
    pair_factor,
    blocks,
    pair_block,
    block_home,
    tile_mask,
    row_energy,
    column_energy,
):
    ny, nx, nz = lax.axis_size("y"), lax.axis_size("x"), lax.axis_size("z")
    pairs, naux, tile = pair_factor.shape
    rows, width = amplitudes.shape
    sem = pltpu.SemaphoreType.DMA

    def ring(value, axis, cross=False, hops=1):
        n = lax.axis_size(axis)
        names, at = (("y", "core"), lambda c, i: i * 2 + c) if axis == "y" else (("core", axis), lambda c, i: c * n + i)
        pairs_of = []
        for to in range(2):
            for i in range(n):
                pairs_of.append((at(1 - to if cross else to, i), at(to, (i + (hops, -hops)[to]) % n)))
        return lax.ppermute(value, names, pairs_of)

    def swap(value):
        return lax.ppermute(value, "core", [(0, 1), (1, 0)])

    def chain(value, axis):
        same, cross = [ring(value, axis)], [ring(value, axis, cross=True)]
        for _ in range(FAR - 2):
            same.append(ring(same[-1], axis))
            cross.append(ring(cross[-1], axis))
        return same, cross

    gathered = lax.all_gather(blocks, ("y", "core"), axis=0, tiled=True)
    factor = jnp.swapaxes(pair_factor, 1, 2)

    amp_same, amp_cross = chain(amplitudes, "z")
    amp_far = ring(amp_same[1], "z", hops=2)

    depth = nz * width
    panels = lax.all_to_all(dressing.reshape(nx, depth, width), "x", 0, 0)
    taken = (FAR + 1) * width
    bf16 = jnp.bfloat16
    shape = jax.ShapeDtypeStruct((nx, rows, width), F32)
    high, low = pl.pallas_call(
        lambda *refs: dressing_kernel(nz, *refs),
        out_shape=[jax.ShapeDtypeStruct((taken, nx * width), bf16)] * 2,
        in_specs=[HBM],
        out_specs=[VMEM] * 2,
        scratch_shapes=[pltpu.VMEM((FAR + 1, nx, width, width), F32), sem((FAR + 1,))],
        compiler_params=PARAMS,
        name="dressing_ready",
    )(panels)

    def product(pieces, first, name, flops, *earlier):
        count, added = len(pieces), len(earlier)
        return pl.pallas_call(
            lambda *refs: product_kernel(first, count, added, *refs),
            out_shape=shape,
            in_specs=[HBM] * (count + 2 + added),
            out_specs=VMEM,
            scratch_shapes=[pltpu.VMEM((count, rows, width), F32)]
            + [pltpu.VMEM((count * width, nx * width), bf16)] * 2
            + [pltpu.VMEM((rows, count * width), bf16)] * 2
            + [sem((count + 2 + added,))]
            + ([pltpu.VMEM((added, nx, rows, width), F32)] if added else []),
            compiler_params=PARAMS,
            cost_estimate=pl.CostEstimate(flops=flops, bytes_accessed=1000000, transcendentals=0),
            name=name,
        )(*pieces, high, low, *earlier)

    count = len(amp_cross)
    slices = pl.pallas_call(
        slices_kernel,
        out_shape=[jax.ShapeDtypeStruct((rows, count * width), bf16)] * 2,
        in_specs=[HBM] * count,
        out_specs=[VMEM] * 2,
        scratch_shapes=[pltpu.VMEM((count, rows, width), F32), sem((count,))],
        compiler_params=PARAMS,
        cost_estimate=pl.CostEstimate(flops=SLICES, bytes_accessed=1000000, transcendentals=0),
        name="slices_ready",
    )(*amp_cross)
    other = pl.pallas_call(
        lambda *refs: other_kernel(1, *refs),
        out_shape=shape,
        in_specs=[HBM] * 4,
        out_specs=VMEM,
        scratch_shapes=[
            pltpu.VMEM((2, rows, count * width), bf16),
            pltpu.VMEM((2, count * width, nx * width), bf16),
            sem((4,)),
        ],
        compiler_params=PARAMS,
        cost_estimate=pl.CostEstimate(flops=OTHER, bytes_accessed=1000000, transcendentals=0),
        name="dressed_other",
    )(*slices, high, low)
    other = swap(other)
    early = product([amplitudes, *amp_same[:2]], 0, "dressed_early", EARLY)
    sums = product([amp_same[2], amp_far], 3, "dressed_late", LATE, early, other)
    sums = lax.all_to_all(sums, "x", 0, 0)

    stacked = pl.pallas_call(
        factor_kernel,
        out_shape=jax.ShapeDtypeStruct((pairs, 2 * tile, naux), bf16),
        in_specs=[VMEM],
        out_specs=VMEM,
        compiler_params=PARAMS,
        name="factor_ready",
    )(factor)
    group = lax.axis_index("y") * 2 + lax.axis_index("core")
    mine = lax.dynamic_slice_in_dim(pair_block, group * pairs, pairs)
    places = jnp.arange(block_home.shape[0], dtype=jnp.int32)
    homes = jnp.sum(jnp.where(mine[:, None] == places, block_home, 0), axis=1)
    where = jnp.concatenate([homes, tile_mask.reshape(-1)])
    integral = pl.pallas_call(
        lambda *refs: integral_kernel(pairs, *refs),
        out_shape=jax.ShapeDtypeStruct((rows, width), F32),
        in_specs=[SMEM, HBM, HBM],
        out_specs=VMEM,
        scratch_shapes=[
            pltpu.VMEM((pairs, 2 * tile, naux), bf16),
            pltpu.VMEM((pairs, naux, width), F32),
            sem((pairs + 1,)),
        ],
        compiler_params=pltpu.CompilerParams(vmem_limit_bytes=48 * 1024 * 1024),
        name="integral",
    )(where, stacked, gathered)
    residual = integral + ((sums[0] + sums[1]) + (sums[2] + sums[3]))
    return residual, amplitudes - residual / (row_energy[:, None] + column_energy[None, :])


def solution(mesh):
    sizes = {"y": 8, "core": 2, "x": 4, "z": 8}
    fine = Mesh(mesh.devices.reshape(tuple(sizes.values())), tuple(sizes))
    grp, row = ("y", "core"), ("x", "z")
    placed = (
        P(grp, row),
        P(None, row),
        P(grp, None, None),
        P(grp, None, row),
        P(),
        P(),
        P(grp, row),
        P(grp),
        P(row),
    )
    return jax.shard_map(
        shards,
        mesh=fine,
        in_specs=placed,
        out_specs=(P(grp, row), P(grp, row)),
        check_vma=False,
    )
```

```python
import jax
import jax.numpy as jnp
from jax import lax
from jax.experimental import pallas as pl
from jax.experimental.pallas import tpu as pltpu
from jax.sharding import Mesh
from jax.sharding import PartitionSpec as P

F32 = jnp.float32
PARAMS = pltpu.CompilerParams(vmem_limit_bytes=20 * 1024 * 1024)
HBM = pl.BlockSpec(memory_space=pltpu.HBM)
VMEM = pl.BlockSpec(memory_space=pltpu.VMEM)
SMEM = pl.BlockSpec(memory_space=pltpu.SMEM)
OTHER = 1000
SLICES = 10000000000
EARLY = 30000000000
LATE = 1000
FAR = 4


def split(value):
    high = value.astype(jnp.bfloat16)
    low = (value - high.astype(F32)).astype(jnp.bfloat16)
    return high, low


def dot3(left, right):
    one = lambda a, b: jnp.dot(a, b, preferred_element_type=F32)
    return one(left[0], right[0]) + (one(left[0], right[1]) + one(left[1], right[0]))


def start_all(copies, sems):
    made = [pltpu.make_async_copy(src, dst, sems.at[i]) for i, (src, dst) in enumerate(copies)]
    for copy in made:
        copy.start()
    return made


def behind(index, size, core, step):
    return lax.rem(index + jnp.where(core == 0, size - step, step), size)


def dressing_kernel(nz, panels, high, low, held, sems):
    count, _, width = panels.shape
    core, z = lax.axis_index("core"), lax.axis_index("z")
    copies = []
    for t in range(FAR + 1):
        row = pl.multiple_of(behind(z, nz, core, t) * width, width)
        copies.append((panels.at[:, pl.ds(row, width)], held.at[t]))
    made = start_all(copies, sems)
    for t in range(FAR + 1):
        made[t].wait()
        for s in range(count):
            at = slice(t * width, (t + 1) * width), slice(s * width, (s + 1) * width)
            high[at], low[at] = split(held[t, s])


def products(out, left, right, plus=None):
    width = out.shape[2]
    for s in range(0, out.shape[0], 2):
        at = slice(s * width, (s + 2) * width)
        both = dot3(left, (right[0][:, at], right[1][:, at]))
        for k in range(2):
            value = both[:, k * width : (k + 1) * width]
            out[s + k] = value if plus is None else value + plus(s + k)


def product_kernel(first, count, added, *refs):
    pieces, high, low, refs = refs[:count], refs[count], refs[count + 1], refs[count + 2 :]
    earlier, refs = refs[:added], refs[added:]
    out, held, right_high, right_low, left_high, left_low, sems = refs[:7]
    width = held.shape[2]
    rows = pl.ds(first * width, count * width)
    copies = [(piece, held.at[k]) for k, piece in enumerate(pieces)]
    copies += [(high.at[rows], right_high), (low.at[rows], right_low)]
    copies += [(ref, refs[7].at[k]) for k, ref in enumerate(earlier)]
    made = start_all(copies, sems)
    for k in range(count):
        made[k].wait()
        at = slice(k * width, (k + 1) * width)
        left_high[:, at], left_low[:, at] = split(held[k])
    for copy in made[count:]:
        copy.wait()
    plus = (lambda s: refs[7][0, s] + refs[7][1, s]) if added else None
    products(out, (left_high[...], left_low[...]), (right_high, right_low), plus)


def slices_kernel(*refs):
    count = len(refs) - 4
    pieces, (high, low, held, sems) = refs[:count], refs[count:]
    width = held.shape[2]
    made = start_all([(piece, held.at[k]) for k, piece in enumerate(pieces)], sems)
    for k in range(count):
        made[k].wait()
        at = slice(k * width, (k + 1) * width)
        high[:, at], low[:, at] = split(held[k])


def other_kernel(first, left_high, left_low, high, low, out, lefts, rights, sems):
    width = out.shape[2]
    rows = pl.ds(first * width, rights.shape[1])
    copies = [(left_high, lefts.at[0]), (left_low, lefts.at[1])]
    copies += [(high.at[rows], rights.at[0]), (low.at[rows], rights.at[1])]
    for copy in start_all(copies, sems):
        copy.wait()
    products(out, (lefts[0], lefts[1]), (rights.at[0], rights.at[1]))


def factor_kernel(factor, stacked):
    tile = factor.shape[1]
    for i in range(factor.shape[0]):
        high, low = split(factor[i])
        stacked[i, :tile] = high
        stacked[i, tile:] = low


def block_at(gathered, home):
    return gathered.at[home]


def integral_kernel(pairs, where, factors, gathered, out, blocks, sems):
    made = [
        pltpu.make_async_copy(block_at(gathered, where[i]), blocks.at[i], sems.at[i]) for i in range(pairs)
    ]
    for i in range(pairs):
        made[i].start(priority=i % 2)
    for copy in made:
        copy.wait()
    tile = factors.shape[1] // 2
    width = out.shape[1]
    lane = lax.broadcasted_iota(jnp.int32, (tile, width), 1)
    for i in range(pairs):
        both = jnp.dot(factors[i], jnp.concatenate(split(blocks[i]), axis=1), preferred_element_type=F32)
        integral = both[:tile, :width] + (both[tile:, :width] + both[:tile, width:])
        on = jnp.where(lane < tile, where[pairs + 2 * i], where[pairs + 2 * i + 1]).astype(F32)
        out[i * tile : (i + 1) * tile] = integral * on


def shards(
    amplitudes,
    dressing,
    pair_factor,
    blocks,
    pair_block,
    block_home,
    tile_mask,
    row_energy,
    column_energy,
):
    ny, nx, nz = lax.axis_size("y"), lax.axis_size("x"), lax.axis_size("z")
    pairs, naux, tile = pair_factor.shape
    rows, width = amplitudes.shape
    sem = pltpu.SemaphoreType.DMA

    def ring(value, axis, cross=False, hops=1):
        n = lax.axis_size(axis)
        names, at = (("y", "core"), lambda c, i: i * 2 + c) if axis == "y" else (("core", axis), lambda c, i: c * n + i)
        pairs_of = []
        for to in range(2):
            for i in range(n):
                pairs_of.append((at(1 - to if cross else to, i), at(to, (i + (hops, -hops)[to]) % n)))
        return lax.ppermute(value, names, pairs_of)

    def swap(value):
        return lax.ppermute(value, "core", [(0, 1), (1, 0)])

    def chain(value, axis):
        same, cross = [ring(value, axis)], [ring(value, axis, cross=True)]
        for _ in range(FAR - 2):
            same.append(ring(same[-1], axis))
            cross.append(ring(cross[-1], axis))
        return same, cross

    gathered = lax.all_gather(blocks, ("y", "core"), axis=0, tiled=True)
    factor = jnp.swapaxes(pair_factor, 1, 2)

    amp_same, amp_cross = chain(amplitudes, "z")
    amp_far = ring(amp_same[1], "z", hops=2)

    depth = nz * width
    panels = lax.all_to_all(dressing.reshape(nx, depth, width), "x", 0, 0)
    taken = (FAR + 1) * width
    bf16 = jnp.bfloat16
    shape = jax.ShapeDtypeStruct((nx, rows, width), F32)
    high, low = pl.pallas_call(
        lambda *refs: dressing_kernel(nz, *refs),
        out_shape=[jax.ShapeDtypeStruct((taken, nx * width), bf16)] * 2,
        in_specs=[HBM],
        out_specs=[VMEM] * 2,
        scratch_shapes=[pltpu.VMEM((FAR + 1, nx, width, width), F32), sem((FAR + 1,))],
        compiler_params=PARAMS,
        name="dressing_ready",
    )(panels)

    def product(pieces, first, name, flops, *earlier):
        count, added = len(pieces), len(earlier)
        return pl.pallas_call(
            lambda *refs: product_kernel(first, count, added, *refs),
            out_shape=shape,
            in_specs=[HBM] * (count + 2 + added),
            out_specs=VMEM,
            scratch_shapes=[pltpu.VMEM((count, rows, width), F32)]
            + [pltpu.VMEM((count * width, nx * width), bf16)] * 2
            + [pltpu.VMEM((rows, count * width), bf16)] * 2
            + [sem((count + 2 + added,))]
            + ([pltpu.VMEM((added, nx, rows, width), F32)] if added else []),
            compiler_params=PARAMS,
            cost_estimate=pl.CostEstimate(flops=flops, bytes_accessed=1000000, transcendentals=0),
            name=name,
        )(*pieces, high, low, *earlier)

    count = len(amp_cross)
    slices = pl.pallas_call(
        slices_kernel,
        out_shape=[jax.ShapeDtypeStruct((rows, count * width), bf16)] * 2,
        in_specs=[HBM] * count,
        out_specs=[VMEM] * 2,
        scratch_shapes=[pltpu.VMEM((count, rows, width), F32), sem((count,))],
        compiler_params=PARAMS,
        cost_estimate=pl.CostEstimate(flops=SLICES, bytes_accessed=1000000, transcendentals=0),
        name="slices_ready",
    )(*amp_cross)
    other = pl.pallas_call(
        lambda *refs: other_kernel(1, *refs),
        out_shape=shape,
        in_specs=[HBM] * 4,
        out_specs=VMEM,
        scratch_shapes=[
            pltpu.VMEM((2, rows, count * width), bf16),
            pltpu.VMEM((2, count * width, nx * width), bf16),
            sem((4,)),
        ],
        compiler_params=PARAMS,
        cost_estimate=pl.CostEstimate(flops=OTHER, bytes_accessed=1000000, transcendentals=0),
        name="dressed_other",
    )(*slices, high, low)
    other = swap(other)
    early = product([amplitudes, *amp_same[:2]], 0, "dressed_early", EARLY)
    sums = product([amp_same[2], amp_far], 3, "dressed_late", LATE, early, other)
    sums = lax.all_to_all(sums, "x", 0, 0)

    stacked = pl.pallas_call(
        factor_kernel,
        out_shape=jax.ShapeDtypeStruct((pairs, 2 * tile, naux), bf16),
        in_specs=[VMEM],
        out_specs=VMEM,
        compiler_params=PARAMS,
        name="factor_ready",
    )(factor)
    group = lax.axis_index("y") * 2 + lax.axis_index("core")
    mine = lax.dynamic_slice_in_dim(pair_block, group * pairs, pairs)
    places = jnp.arange(block_home.shape[0], dtype=jnp.int32)
    homes = jnp.sum(jnp.where(mine[:, None] == places, block_home, 0), axis=1)
    where = jnp.concatenate([homes, tile_mask.reshape(-1)])
    integral = pl.pallas_call(
        lambda *refs: integral_kernel(pairs, *refs),
        out_shape=jax.ShapeDtypeStruct((rows, width), F32),
        grid_spec=pltpu.PrefetchScalarGridSpec(
            num_scalar_prefetch=1,
            grid=(),
            in_specs=[VMEM, HBM],
            out_specs=VMEM,
            scratch_shapes=[pltpu.VMEM((pairs, naux, width), F32), sem((pairs,))],
        ),
        compiler_params=pltpu.CompilerParams(vmem_limit_bytes=48 * 1024 * 1024),
        name="integral",
    )(where, stacked, gathered)
    residual = integral + ((sums[0] + sums[1]) + (sums[2] + sums[3]))
    return residual, amplitudes - residual / (row_energy[:, None] + column_energy[None, :])


def solution(mesh):
    sizes = {"y": 8, "core": 2, "x": 4, "z": 8}
    fine = Mesh(mesh.devices.reshape(tuple(sizes.values())), tuple(sizes))
    grp, row = ("y", "core"), ("x", "z")
    placed = (
        P(grp, row),
        P(None, row),
        P(grp, None, None),
        P(grp, None, row),
        P(),
        P(),
        P(grp, row),
        P(grp),
        P(row),
    )
    return jax.shard_map(
        shards,
        mesh=fine,
        in_specs=placed,
        out_specs=(P(grp, row), P(grp, row)),
        check_vma=False,
    )
```

```python
import jax
import jax.numpy as jnp
from jax import lax
from jax.experimental import pallas as pl
from jax.experimental.pallas import tpu as pltpu
from jax.sharding import Mesh
from jax.sharding import PartitionSpec as P

F32 = jnp.float32
PARAMS = pltpu.CompilerParams(vmem_limit_bytes=20 * 1024 * 1024)
HBM = pl.BlockSpec(memory_space=pltpu.HBM)
VMEM = pl.BlockSpec(memory_space=pltpu.VMEM)
SMEM = pl.BlockSpec(memory_space=pltpu.SMEM)
OTHER = 1000
SLICES = 10000000000
EARLY = 30000000000
LATE = 1000
FAR = 4


def split(value):
    high = value.astype(jnp.bfloat16)
    low = (value - high.astype(F32)).astype(jnp.bfloat16)
    return high, low


def dot3(left, right):
    one = lambda a, b: jnp.dot(a, b, preferred_element_type=F32)
    return one(left[0], right[0]) + (one(left[0], right[1]) + one(left[1], right[0]))


def start_all(copies, sems):
    made = [pltpu.make_async_copy(src, dst, sems.at[i]) for i, (src, dst) in enumerate(copies)]
    for copy in made:
        copy.start()
    return made


def behind(index, size, core, step):
    return lax.rem(index + jnp.where(core == 0, size - step, step), size)


def dressing_kernel(nz, panels, high, low, held, sems):
    count, _, width = panels.shape
    core, z = lax.axis_index("core"), lax.axis_index("z")
    copies = []
    for t in range(FAR + 1):
        row = pl.multiple_of(behind(z, nz, core, t) * width, width)
        copies.append((panels.at[:, pl.ds(row, width)], held.at[t]))
    made = start_all(copies, sems)
    for t in range(FAR + 1):
        made[t].wait()
        for s in range(count):
            at = slice(t * width, (t + 1) * width), slice(s * width, (s + 1) * width)
            high[at], low[at] = split(held[t, s])


def products(out, left, right, plus=None):
    width = out.shape[2]
    for s in range(0, out.shape[0], 2):
        at = slice(s * width, (s + 2) * width)
        both = dot3(left, (right[0][:, at], right[1][:, at]))
        for k in range(2):
            value = both[:, k * width : (k + 1) * width]
            out[s + k] = value if plus is None else value + plus(s + k)


def product_kernel(first, count, added, last_first, *refs):
    pieces, high, low, refs = refs[:count], refs[count], refs[count + 1], refs[count + 2 :]
    earlier, refs = refs[:added], refs[added:]
    out, held, right_high, right_low, left_high, left_low, sems = refs[:7]
    width = held.shape[2]
    rows = pl.ds(first * width, count * width)
    copies = [(piece, held.at[k]) for k, piece in enumerate(pieces)]
    copies += [(high.at[rows], right_high), (low.at[rows], right_low)]
    copies += [(ref, refs[7].at[k]) for k, ref in enumerate(earlier)]
    made = start_all(copies, sems)
    for k in range(count):
        made[k].wait()
        step = count - 1 - k if last_first else k
        at = slice(step * width, (step + 1) * width)
        left_high[:, at], left_low[:, at] = split(held[k])
    for copy in made[count:]:
        copy.wait()
    plus = (lambda s: refs[7][0, s] + refs[7][1, s]) if added else None
    products(out, (left_high[...], left_low[...]), (right_high, right_low), plus)


def slices_kernel(*refs):
    count = len(refs) - 4
    pieces, (high, low, held, sems) = refs[:count], refs[count:]
    width = held.shape[2]
    made = start_all([(piece, held.at[k]) for k, piece in enumerate(pieces)], sems)
    for k in range(count):
        made[k].wait()
        at = slice(k * width, (k + 1) * width)
        high[:, at], low[:, at] = split(held[k])


def other_kernel(first, left_high, left_low, high, low, out, lefts, rights, sems):
    width = out.shape[2]
    rows = pl.ds(first * width, rights.shape[1])
    copies = [(left_high, lefts.at[0]), (left_low, lefts.at[1])]
    copies += [(high.at[rows], rights.at[0]), (low.at[rows], rights.at[1])]
    for copy in start_all(copies, sems):
        copy.wait()
    products(out, (lefts[0], lefts[1]), (rights.at[0], rights.at[1]))


def factor_kernel(factor, stacked):
    tile = factor.shape[1]
    for i in range(factor.shape[0]):
        high, low = split(factor[i])
        stacked[i, :tile] = high
        stacked[i, tile:] = low


def block_at(gathered, home):
    return gathered.at[home]


def integral_kernel(pairs, where, stacked, gathered, out, factors, blocks, sems):
    made = start_all(
        [(block_at(gathered, where[i]), blocks.at[i]) for i in range(pairs)] + [(stacked, factors)], sems
    )
    for copy in made:
        copy.wait()
    tile = factors.shape[1] // 2
    width = out.shape[1]
    lane = lax.broadcasted_iota(jnp.int32, (tile, width), 1)
    for i in range(pairs):
        both = jnp.dot(factors[i], jnp.concatenate(split(blocks[i]), axis=1), preferred_element_type=F32)
        integral = both[:tile, :width] + (both[tile:, :width] + both[:tile, width:])
        on = jnp.where(lane < tile, where[pairs + 2 * i], where[pairs + 2 * i + 1]).astype(F32)
        out[i * tile : (i + 1) * tile] = integral * on


def shards(
    amplitudes,
    dressing,
    pair_factor,
    blocks,
    pair_block,
    block_home,
    tile_mask,
    row_energy,
    column_energy,
):
    ny, nx, nz = lax.axis_size("y"), lax.axis_size("x"), lax.axis_size("z")
    pairs, naux, tile = pair_factor.shape
    rows, width = amplitudes.shape
    sem = pltpu.SemaphoreType.DMA

    def ring(value, axis, cross=False, hops=1):
        n = lax.axis_size(axis)
        names, at = (("y", "core"), lambda c, i: i * 2 + c) if axis == "y" else (("core", axis), lambda c, i: c * n + i)
        pairs_of = []
        for to in range(2):
            for i in range(n):
                pairs_of.append((at(1 - to if cross else to, i), at(to, (i + (hops, -hops)[to]) % n)))
        return lax.ppermute(value, names, pairs_of)

    def swap(value):
        return lax.ppermute(value, "core", [(0, 1), (1, 0)])

    def chain(value, axis):
        same, cross = [ring(value, axis)], [ring(value, axis, cross=True)]
        for _ in range(FAR - 2):
            same.append(ring(same[-1], axis))
            cross.append(ring(cross[-1], axis))
        return same, cross

    gathered = lax.all_gather(blocks, ("y", "core"), axis=0, tiled=True)
    factor = jnp.swapaxes(pair_factor, 1, 2)

    amp_same, amp_cross = chain(amplitudes, "z")
    amp_far = ring(amp_same[1], "z", hops=2)

    depth = nz * width
    panels = lax.all_to_all(dressing.reshape(nx, depth, width), "x", 0, 0)
    taken = (FAR + 1) * width
    bf16 = jnp.bfloat16
    shape = jax.ShapeDtypeStruct((nx, rows, width), F32)
    high, low = pl.pallas_call(
        lambda *refs: dressing_kernel(nz, *refs),
        out_shape=[jax.ShapeDtypeStruct((taken, nx * width), bf16)] * 2,
        in_specs=[HBM],
        out_specs=[VMEM] * 2,
        scratch_shapes=[pltpu.VMEM((FAR + 1, nx, width, width), F32), sem((FAR + 1,))],
        compiler_params=PARAMS,
        name="dressing_ready",
    )(panels)

    def product(pieces, first, name, flops, *earlier, last_first=False):
        count, added = len(pieces), len(earlier)
        return pl.pallas_call(
            lambda *refs: product_kernel(first, count, added, last_first, *refs),
            out_shape=shape,
            in_specs=[HBM] * (count + 2 + added),
            out_specs=VMEM,
            scratch_shapes=[pltpu.VMEM((count, rows, width), F32)]
            + [pltpu.VMEM((count * width, nx * width), bf16)] * 2
            + [pltpu.VMEM((rows, count * width), bf16)] * 2
            + [sem((count + 2 + added,))]
            + ([pltpu.VMEM((added, nx, rows, width), F32)] if added else []),
            compiler_params=PARAMS,
            cost_estimate=pl.CostEstimate(flops=flops, bytes_accessed=1000000, transcendentals=0),
            name=name,
        )(*pieces, high, low, *earlier)

    count = len(amp_cross)
    slices = pl.pallas_call(
        slices_kernel,
        out_shape=[jax.ShapeDtypeStruct((rows, count * width), bf16)] * 2,
        in_specs=[HBM] * count,
        out_specs=[VMEM] * 2,
        scratch_shapes=[pltpu.VMEM((count, rows, width), F32), sem((count,))],
        compiler_params=PARAMS,
        cost_estimate=pl.CostEstimate(flops=SLICES, bytes_accessed=1000000, transcendentals=0),
        name="slices_ready",
    )(*amp_cross)
    other = pl.pallas_call(
        lambda *refs: other_kernel(1, *refs),
        out_shape=shape,
        in_specs=[HBM] * 4,
        out_specs=VMEM,
        scratch_shapes=[
            pltpu.VMEM((2, rows, count * width), bf16),
            pltpu.VMEM((2, count * width, nx * width), bf16),
            sem((4,)),
        ],
        compiler_params=PARAMS,
        cost_estimate=pl.CostEstimate(flops=OTHER, bytes_accessed=1000000, transcendentals=0),
        name="dressed_other",
    )(*slices, high, low)
    other = swap(other)
    early = product([amplitudes, *amp_same[:2]], 0, "dressed_early", EARLY)
    sums = product([amp_far, amp_same[2]], 3, "dressed_late", LATE, early, other, last_first=True)
    sums = lax.all_to_all(sums, "x", 0, 0)

    stacked = pl.pallas_call(
        factor_kernel,
        out_shape=jax.ShapeDtypeStruct((pairs, 2 * tile, naux), bf16),
        in_specs=[VMEM],
        out_specs=VMEM,
        compiler_params=PARAMS,
        name="factor_ready",
    )(factor)
    group = lax.axis_index("y") * 2 + lax.axis_index("core")
    mine = lax.dynamic_slice_in_dim(pair_block, group * pairs, pairs)
    places = jnp.arange(block_home.shape[0], dtype=jnp.int32)
    homes = jnp.sum(jnp.where(mine[:, None] == places, block_home, 0), axis=1)
    where = jnp.concatenate([homes, tile_mask.reshape(-1)])
    integral = pl.pallas_call(
        lambda *refs: integral_kernel(pairs, *refs),
        out_shape=jax.ShapeDtypeStruct((rows, width), F32),
        in_specs=[SMEM, HBM, HBM],
        out_specs=VMEM,
        scratch_shapes=[
            pltpu.VMEM((pairs, 2 * tile, naux), bf16),
            pltpu.VMEM((pairs, naux, width), F32),
            sem((pairs + 1,)),
        ],
        compiler_params=pltpu.CompilerParams(vmem_limit_bytes=48 * 1024 * 1024),
        name="integral",
    )(where, stacked, gathered)
    residual = integral + ((sums[0] + sums[1]) + (sums[2] + sums[3]))
    return residual, amplitudes - residual / (row_energy[:, None] + column_energy[None, :])


def solution(mesh):
    sizes = {"y": 8, "core": 2, "x": 4, "z": 8}
    fine = Mesh(mesh.devices.reshape(tuple(sizes.values())), tuple(sizes))
    grp, row = ("y", "core"), ("x", "z")
    placed = (
        P(grp, row),
        P(None, row),
        P(grp, None, None),
        P(grp, None, row),
        P(),
        P(),
        P(grp, row),
        P(grp),
        P(row),
    )
    return jax.shard_map(
        shards,
        mesh=fine,
        in_specs=placed,
        out_specs=(P(grp, row), P(grp, row)),
        check_vma=False,
    )
```

```python
import jax
import jax.numpy as jnp
from jax import lax
from jax.experimental import pallas as pl
from jax.experimental.pallas import tpu as pltpu
from jax.sharding import Mesh
from jax.sharding import PartitionSpec as P

F32 = jnp.float32
PARAMS = pltpu.CompilerParams(vmem_limit_bytes=20 * 1024 * 1024)
HBM = pl.BlockSpec(memory_space=pltpu.HBM)
VMEM = pl.BlockSpec(memory_space=pltpu.VMEM)
SMEM = pl.BlockSpec(memory_space=pltpu.SMEM)
OTHER = 1000
SLICES = 10000000000
EARLY = 30000000000
LATE = 1000
FAR = 4


def split(value):
    high = value.astype(jnp.bfloat16)
    low = (value - high.astype(F32)).astype(jnp.bfloat16)
    return high, low


def dot3(left, right):
    one = lambda a, b: jnp.dot(a, b, preferred_element_type=F32)
    return one(left[0], right[0]) + (one(left[0], right[1]) + one(left[1], right[0]))


def start_all(copies, sems):
    made = [pltpu.make_async_copy(src, dst, sems.at[i]) for i, (src, dst) in enumerate(copies)]
    for copy in made:
        copy.start()
    return made


def behind(index, size, core, step):
    return lax.rem(index + jnp.where(core == 0, size - step, step), size)


def dressing_kernel(nz, panels, high, low, held, sems):
    count, _, width = panels.shape
    core, z = lax.axis_index("core"), lax.axis_index("z")
    copies = []
    for t in range(FAR + 1):
        row = pl.multiple_of(behind(z, nz, core, t) * width, width)
        copies.append((panels.at[:, pl.ds(row, width)], held.at[t]))
    made = start_all(copies, sems)
    for t in range(FAR + 1):
        made[t].wait()
        for s in range(count):
            at = slice(t * width, (t + 1) * width), slice(s * width, (s + 1) * width)
            high[at], low[at] = split(held[t, s])


def products(out, left, right, plus=None):
    width = out.shape[2]
    for s in range(0, out.shape[0], 2):
        at = slice(s * width, (s + 2) * width)
        both = dot3(left, (right[0][:, at], right[1][:, at]))
        for k in range(2):
            value = both[:, k * width : (k + 1) * width]
            out[s + k] = value if plus is None else value + plus(s + k)


def product_kernel(first, count, added, last_first, *refs):
    pieces, high, low, refs = refs[:count], refs[count], refs[count + 1], refs[count + 2 :]
    earlier, refs = refs[:added], refs[added:]
    out, held, right_high, right_low, left_high, left_low, sems = refs[:7]
    width = held.shape[2]
    rows = pl.ds(first * width, count * width)
    copies = [(piece, held.at[k]) for k, piece in enumerate(pieces)]
    copies += [(high.at[rows], right_high), (low.at[rows], right_low)]
    copies += [(ref, refs[7].at[k]) for k, ref in enumerate(earlier)]
    made = start_all(copies, sems)
    for k in range(count):
        made[k].wait()
        step = count - 1 - k if last_first else k
        at = slice(step * width, (step + 1) * width)
        left_high[:, at], left_low[:, at] = split(held[k])
    for copy in made[count:]:
        copy.wait()
    plus = (lambda s: refs[7][0, s] + refs[7][1, s]) if added else None
    products(out, (left_high[...], left_low[...]), (right_high, right_low), plus)


def slices_kernel(*refs):
    count = len(refs) - 4
    pieces, (high, low, held, sems) = refs[:count], refs[count:]
    width = held.shape[2]
    made = start_all([(piece, held.at[k]) for k, piece in enumerate(pieces)], sems)
    for k in range(count):
        made[k].wait()
        at = slice(k * width, (k + 1) * width)
        high[:, at], low[:, at] = split(held[k])


def other_kernel(first, left_high, left_low, high, low, out, lefts, rights, sems):
    width = out.shape[2]
    rows = pl.ds(first * width, rights.shape[1])
    copies = [(left_high, lefts.at[0]), (left_low, lefts.at[1])]
    copies += [(high.at[rows], rights.at[0]), (low.at[rows], rights.at[1])]
    for copy in start_all(copies, sems):
        copy.wait()
    products(out, (lefts[0], lefts[1]), (rights.at[0], rights.at[1]))


def factor_kernel(factor, stacked):
    tile = factor.shape[1]
    for i in range(factor.shape[0]):
        high, low = split(factor[i])
        stacked[i, :tile] = high
        stacked[i, tile:] = low


def block_at(gathered, home):
    return gathered.at[home]


def integral_kernel(pairs, where, factors, gathered, out, blocks, sems):
    made = [
        pltpu.make_async_copy(block_at(gathered, where[i]), blocks.at[i], sems.at[i]) for i in range(pairs)
    ]
    for i in range(pairs):
        made[i].start(priority=i % 2)
    for copy in made:
        copy.wait()
    tile = factors.shape[1] // 2
    width = out.shape[1]
    lane = lax.broadcasted_iota(jnp.int32, (tile, width), 1)
    for i in range(pairs):
        both = jnp.dot(factors[i], jnp.concatenate(split(blocks[i]), axis=1), preferred_element_type=F32)
        integral = both[:tile, :width] + (both[tile:, :width] + both[:tile, width:])
        on = jnp.where(lane < tile, where[pairs + 2 * i], where[pairs + 2 * i + 1]).astype(F32)
        out[i * tile : (i + 1) * tile] = integral * on


def shards(
    amplitudes,
    dressing,
    pair_factor,
    blocks,
    pair_block,
    block_home,
    tile_mask,
    row_energy,
    column_energy,
):
    ny, nx, nz = lax.axis_size("y"), lax.axis_size("x"), lax.axis_size("z")
    pairs, naux, tile = pair_factor.shape
    rows, width = amplitudes.shape
    sem = pltpu.SemaphoreType.DMA

    def ring(value, axis, cross=False, hops=1):
        n = lax.axis_size(axis)
        names, at = (("y", "core"), lambda c, i: i * 2 + c) if axis == "y" else (("core", axis), lambda c, i: c * n + i)
        pairs_of = []
        for to in range(2):
            for i in range(n):
                pairs_of.append((at(1 - to if cross else to, i), at(to, (i + (hops, -hops)[to]) % n)))
        return lax.ppermute(value, names, pairs_of)

    def swap(value):
        return lax.ppermute(value, "core", [(0, 1), (1, 0)])

    def chain(value, axis):
        same, cross = [ring(value, axis)], [ring(value, axis, cross=True)]
        for _ in range(FAR - 2):
            same.append(ring(same[-1], axis))
            cross.append(ring(cross[-1], axis))
        return same, cross

    gathered = lax.all_gather(blocks, ("y", "core"), axis=0, tiled=True)
    factor = jnp.swapaxes(pair_factor, 1, 2)

    amp_same, amp_cross = chain(amplitudes, "z")
    amp_far = ring(amp_same[1], "z", hops=2)

    depth = nz * width
    panels = lax.all_to_all(dressing.reshape(nx, depth, width), "x", 0, 0)
    taken = (FAR + 1) * width
    bf16 = jnp.bfloat16
    shape = jax.ShapeDtypeStruct((nx, rows, width), F32)
    high, low = pl.pallas_call(
        lambda *refs: dressing_kernel(nz, *refs),
        out_shape=[jax.ShapeDtypeStruct((taken, nx * width), bf16)] * 2,
        in_specs=[HBM],
        out_specs=[VMEM] * 2,
        scratch_shapes=[pltpu.VMEM((FAR + 1, nx, width, width), F32), sem((FAR + 1,))],
        compiler_params=PARAMS,
        name="dressing_ready",
    )(panels)

    def product(pieces, first, name, flops, *earlier, last_first=False):
        count, added = len(pieces), len(earlier)
        return pl.pallas_call(
            lambda *refs: product_kernel(first, count, added, last_first, *refs),
            out_shape=shape,
            in_specs=[HBM] * (count + 2 + added),
            out_specs=VMEM,
            scratch_shapes=[pltpu.VMEM((count, rows, width), F32)]
            + [pltpu.VMEM((count * width, nx * width), bf16)] * 2
            + [pltpu.VMEM((rows, count * width), bf16)] * 2
            + [sem((count + 2 + added,))]
            + ([pltpu.VMEM((added, nx, rows, width), F32)] if added else []),
            compiler_params=PARAMS,
            cost_estimate=pl.CostEstimate(flops=flops, bytes_accessed=1000000, transcendentals=0),
            name=name,
        )(*pieces, high, low, *earlier)

    count = len(amp_cross)
    slices = pl.pallas_call(
        slices_kernel,
        out_shape=[jax.ShapeDtypeStruct((rows, count * width), bf16)] * 2,
        in_specs=[HBM] * count,
        out_specs=[VMEM] * 2,
        scratch_shapes=[pltpu.VMEM((count, rows, width), F32), sem((count,))],
        compiler_params=PARAMS,
        cost_estimate=pl.CostEstimate(flops=SLICES, bytes_accessed=1000000, transcendentals=0),
        name="slices_ready",
    )(*amp_cross)
    other = pl.pallas_call(
        lambda *refs: other_kernel(1, *refs),
        out_shape=shape,
        in_specs=[HBM] * 4,
        out_specs=VMEM,
        scratch_shapes=[
            pltpu.VMEM((2, rows, count * width), bf16),
            pltpu.VMEM((2, count * width, nx * width), bf16),
            sem((4,)),
        ],
        compiler_params=PARAMS,
        cost_estimate=pl.CostEstimate(flops=OTHER, bytes_accessed=1000000, transcendentals=0),
        name="dressed_other",
    )(*slices, high, low)
    other = swap(other)
    early = product([amplitudes, *amp_same[:2]], 0, "dressed_early", EARLY)
    sums = product([amp_far, amp_same[2]], 3, "dressed_late", LATE, early, other, last_first=True)
    sums = lax.all_to_all(sums, "x", 0, 0)

    stacked = pl.pallas_call(
        factor_kernel,
        out_shape=jax.ShapeDtypeStruct((pairs, 2 * tile, naux), bf16),
        in_specs=[VMEM],
        out_specs=VMEM,
        compiler_params=PARAMS,
        name="factor_ready",
    )(factor)
    group = lax.axis_index("y") * 2 + lax.axis_index("core")
    mine = lax.dynamic_slice_in_dim(pair_block, group * pairs, pairs)
    places = jnp.arange(block_home.shape[0], dtype=jnp.int32)
    homes = jnp.sum(jnp.where(mine[:, None] == places, block_home, 0), axis=1)
    where = jnp.concatenate([homes, tile_mask.reshape(-1)])
    integral = pl.pallas_call(
        lambda *refs: integral_kernel(pairs, *refs),
        out_shape=jax.ShapeDtypeStruct((rows, width), F32),
        grid_spec=pltpu.PrefetchScalarGridSpec(
            num_scalar_prefetch=1,
            grid=(),
            in_specs=[VMEM, HBM],
            out_specs=VMEM,
            scratch_shapes=[pltpu.VMEM((pairs, naux, width), F32), sem((pairs,))],
        ),
        compiler_params=pltpu.CompilerParams(vmem_limit_bytes=48 * 1024 * 1024),
        name="integral",
    )(where, stacked, gathered)
    residual = integral + ((sums[0] + sums[1]) + (sums[2] + sums[3]))
    return residual, amplitudes - residual / (row_energy[:, None] + column_energy[None, :])


def solution(mesh):
    sizes = {"y": 8, "core": 2, "x": 4, "z": 8}
    fine = Mesh(mesh.devices.reshape(tuple(sizes.values())), tuple(sizes))
    grp, row = ("y", "core"), ("x", "z")
    placed = (
        P(grp, row),
        P(None, row),
        P(grp, None, None),
        P(grp, None, row),
        P(),
        P(),
        P(grp, row),
        P(grp),
        P(row),
    )
    return jax.shard_map(
        shards,
        mesh=fine,
        in_specs=placed,
        out_specs=(P(grp, row), P(grp, row)),
        check_vma=False,
    )
```
